256 devices in a mesh: tok: 8 (over z), ch: 32 (over y, x, core).
Axes of the slice: x: 4, y: 4, z: 8, core: 2. Of those that a mesh axis runs over, the one named last changes fastest.
Arguments:
- tokens: bfloat16 [16384, 1024], P('tok', 'ch'), may hold values from -6 to 6
- filter_in: float32 [2, 8, 128, 128], replicated, may hold values from -0.375 to 0.375
- filter_out: float32 [2, 8, 128, 128], replicated, may hold values from -0.375 to 0.375
- up_weight: bfloat16 [1024, 4096], P('ch', 'tok'), may hold values from -0.1875 to 0.1875
- down_weight: bfloat16 [4096, 1024], P('tok', 'ch'), may hold values from -0.09375 to 0.09375
- cotangent: bfloat16 [16384, 1024], P('tok', 'ch'), may hold values from -6 to 6
Outputs:
- mixed: bfloat16 [16384, 1024], P('tok', 'ch')
- grad_tokens: bfloat16 [16384, 1024], P('tok', 'ch')
- grad_up: float32 [1024, 4096], P('ch', 'tok')
- grad_down: float32 [4096, 1024], P('tok', 'ch')
- grad_filter_in: float32 [2, 8, 128, 128], replicated
- grad_filter_out: float32 [2, 8, 128, 128], replicated
The draws below stay inside these ranges and needn't reach their ends.
All inputs are finite; a program needn't handle non-finite values.
Results may differ from the reference program's by a relative error of at most 0.02.
Values may be sent and summed in bfloat16 or wider, within the bound.
A program may use at most 128 MiB of HBM per device.

```python
import jax
import jax.numpy as jnp
from jax import lax

NX = 32
NY = 64
NZ = 8
C = 1024
FF = 4096
NB = 8
BS = 128
TOKENS = 16384


def shard_levels(stream_key, extent, split, low, top_value):
    gain = 1.0
    for dim, parts in split:
        draws = jax.random.uniform(jax.random.fold_in(jax.random.fold_in(stream_key, 6), dim), (parts,), jnp.float32, low / len(split), top_value / len(split))
        gain = gain * jnp.repeat(jnp.exp(draws), extent[dim] // parts).reshape((-1,) + (1,) * (len(extent) - 1 - dim))
    return gain


def centred(own_key, shape, spread, reach, shards=(), held_as=jnp.bfloat16):
    array = jax.random.normal(own_key, shape, jnp.float32) * spread
    if len(shards) > 0:
        array = shard_levels(own_key, shape, shards, -0.22, 0.18) * array
    return jnp.clip(array, min=-reach, max=reach).astype(held_as)


def setup_inputs(seed: int = 0) -> dict:
    arg_keys = jax.random.split(jax.random.key(seed), 7)
    tokens = centred(arg_keys[0], (TOKENS, C), 1.0, 6.0, ((0, 8), (1, 32)))
    filter_in = centred(arg_keys[1], (2, NB, BS, BS), (2 * BS) ** -0.5, 0.375, (), jnp.float32)
    filter_out = centred(arg_keys[2], (2, NB, BS, BS), (2 * BS) ** -0.5, 0.375, (), jnp.float32)
    up_weight = centred(arg_keys[3], (C, FF), C ** -0.5, 0.1875, ((0, 32), (1, 8)))
    down_weight = centred(arg_keys[4], (FF, C), FF ** -0.5, 0.09375, ((0, 8), (1, 32)))
    cotangent = centred(arg_keys[5], (TOKENS, C), 1.0, 6.0, ((0, 8), (1, 32)))
    return dict(tokens=tokens, filter_in=filter_in, filter_out=filter_out, up_weight=up_weight, down_weight=down_weight, cotangent=cotangent)


def gelu_tanh(values):
    return jax.nn.gelu(values, approximate=True)

def complex_layer(real_part, imag_part, weight):

    def contract(values, matrix):
        return jnp.einsum('xyznb,nbd->xyznd', values, matrix, precision=lax.Precision.HIGHEST)
    first = contract(real_part, weight[0]) - contract(imag_part, weight[1])
    second = contract(real_part, weight[1]) + contract(imag_part, weight[0])
    return (first, second)

def spectral(signal, filter_in, filter_out):
    grid = signal.reshape(NX, NY, NZ, C)
    spectrum = jnp.fft.fftn(grid, axes=(0, 1, 2), norm='ortho')
    real_part = jnp.real(spectrum).reshape(NX, NY, NZ, NB, BS)
    imag_part = jnp.imag(spectrum).reshape(NX, NY, NZ, NB, BS)
    real_part, imag_part = complex_layer(real_part, imag_part, filter_in)
    real_part, imag_part = complex_layer(gelu_tanh(real_part), gelu_tanh(imag_part), filter_out)
    joined = lax.complex(real_part, imag_part).reshape(NX, NY, NZ, C)
    back = jnp.fft.ifftn(joined, axes=(0, 1, 2), norm='ortho')
    return jnp.real(back).reshape(NX * NY * NZ, C)

def reference(tokens, filter_in, filter_out, up_weight, down_weight, cotangent):
    signal = tokens.astype(jnp.float32)
    branch, spectral_vjp = jax.vjp(spectral, signal, filter_in, filter_out)
    middle = (signal + branch).astype(jnp.bfloat16)
    pre_hidden = jnp.dot(middle, up_weight, preferred_element_type=jnp.float32)
    activated, gelu_vjp = jax.vjp(gelu_tanh, pre_hidden)
    hidden = activated.astype(jnp.bfloat16)
    projected = jnp.dot(hidden, down_weight, preferred_element_type=jnp.float32)
    mixed = (middle.astype(jnp.float32) + projected).astype(jnp.bfloat16)
    back_hidden = jnp.dot(cotangent, down_weight.T, preferred_element_type=jnp.float32)
    grad_down = jnp.dot(hidden.T, cotangent, preferred_element_type=jnp.float32)
    grad_pre = gelu_vjp(back_hidden)[0].astype(jnp.bfloat16)
    grad_up = jnp.dot(middle.T, grad_pre, preferred_element_type=jnp.float32)
    grad_middle = cotangent.astype(jnp.float32) + jnp.dot(grad_pre, up_weight.T, preferred_element_type=jnp.float32)
    spectral_grad, grad_filter_in, grad_filter_out = spectral_vjp(grad_middle)
    grad_tokens = (grad_middle + spectral_grad).astype(jnp.bfloat16)
    return (mixed, grad_tokens, grad_up, grad_down, grad_filter_in, grad_filter_out)
```

```python
import functools
import math

import jax
import jax.numpy as jnp
import ml_dtypes
import numpy as np
from jax import lax
from jax.experimental import pallas as pl
from jax.experimental.pallas import tpu as pltpu
from jax.sharding import PartitionSpec as P

NY = 64
NZ = 8
QG = 4
STRIDE = 11
LANES = 128

f32 = jnp.float32
bf16 = jnp.bfloat16
HIGHEST = lax.Precision.HIGHEST
MESH = pl.DeviceIdType.MESH


@functools.lru_cache(None)
def tables(nz, planes):
    groups = nz * QG
    nx = nz * planes
    plane = NY * NZ
    singles = [(0, 0), (0, NZ // 2), (NY // 2, 0), (NY // 2, NZ // 2)]
    pairs = []
    for v in range(NY):
        for w in range(NZ):
            other = ((-v) % NY, (-w) % NZ)
            if (v, w) < other:
                pairs.append((v, w))
    j = np.repeat(np.arange(NY), NZ)
    k = np.tile(np.arange(NZ), NY)
    rows = []
    for v, w in singles:
        rows.append(np.cos(2 * np.pi * (v * j / NY + w * k / NZ)))
    for v, w in pairs:
        angle = 2 * np.pi * (((v * j) % NY) / NY + ((w * k) % NZ) / NZ)
        rows.append(np.cos(angle))
        rows.append(-np.sin(angle))
    full = np.stack(rows) / math.sqrt(plane)
    assert full.shape == (plane, plane)
    high = full.astype(ml_dtypes.bfloat16)
    low = (full - high.astype(np.float64)).astype(ml_dtypes.bfloat16)
    u = np.arange(nx)
    turn = 2 * np.pi * ((u[:, None] * u[None, :]) % nx) / nx
    cos, sin = np.cos(turn) / math.sqrt(nx), np.sin(turn) / math.sqrt(nx)
    pair = np.zeros((2, nx, 2, 2, nx))
    pair[0, :, 0, 0], pair[0, :, 0, 1] = cos, sin
    pair[1, :, 0, 0], pair[1, :, 0, 1] = -sin, cos
    pair[0, :, 1, 0], pair[0, :, 1, 1] = cos, sin
    pair[1, :, 1, 0], pair[1, :, 1, 1] = sin, -cos
    two = np.zeros((2, nx, 2, 2, nx))
    two[0, :, 0, 0], two[1, :, 0, 0] = cos, -sin
    two[0, :, 1, 1], two[1, :, 1, 1] = cos, -sin

    def ordered(table):
        table = table.reshape(4 * nx, 2, nz, planes).transpose(0, 3, 1, 2)
        return table.reshape(4 * nx, 2 * nx).astype(np.float32)

    width = LANES // QG
    lane = np.zeros((QG * LANES, QG * LANES), np.float32)
    for q in range(QG):
        for i in range(planes):
            for c in range(width):
                lane[q * LANES + i * width + c, i * LANES + q * width + c] = 1.0
    comps = plane // groups
    row = np.zeros((nz * comps, nz * comps), np.float32)
    for z in range(nz):
        for r in range(comps):
            row[r * nz + z, z * comps + r] = 1.0
    return dict(
        high=high,
        low=low,
        pair=ordered(pair),
        two=ordered(two),
        lane=lane.astype(ml_dtypes.bfloat16),
        row=row.astype(ml_dtypes.bfloat16),
    )


def dot(a, b, ca=1, cb=0, precision=None):
    return lax.dot_general(
        a, b, (((ca,), (cb,)), ((), ())), precision=precision, preferred_element_type=f32
    )


SCALE = math.sqrt(2.0 / math.pi)
CUBIC = 0.044715


def gelu(x):
    t = jnp.tanh(SCALE * (x + CUBIC * (x * x * x)))
    return 0.5 * x * (1.0 + t)


def gelu_slope(x):
    t = jnp.tanh(SCALE * (x + CUBIC * (x * x * x)))
    return 0.5 * (1.0 + t) + 0.5 * x * (1.0 - t * t) * (SCALE * (1.0 + 3.0 * CUBIC * (x * x)))


def split(x):
    high = x.astype(bf16)
    return high, (x - high.astype(f32)).astype(bf16)


def kernel(
    nz, nc, planes,
    tokens_in, cotangent_in, up_in, down_in, filter_in, filter_out,
    plh_in, pll_in, mg_in, mt_in, lane_in, row_in,
    mixed, gtok, gup, gdn, gfi, gfo,
    a1s, a1r, a2s, a2r, a3s, a3r, a4s, a4r,
    xs, as_, fil, toks_t, cts, wts,
    mid, midg, cotg, wb, back, hid, gpre,
    gms, gmx, gmh, gmr, prs, prx, prh, prr, gw, gr1, gs, gr2,
    gfs, gfr, gfp, gfz, gfall,
    tokens, cotangent, plh, pll, mg, mt, lane, row,
    send, recv, local,
):
    ny = planes
    nh = nc // ny
    ng = nz * QG
    nb = nc // QG
    nx = nz * planes
    comps = a1s.shape[1]
    cols = comps // 2
    width, plane = wts.shape[1], mid.shape[3]
    hidden = hid.shape[0]
    z = lax.axis_index("tok")
    c = lax.axis_index("ch")
    y, h = c // nh, lax.rem(c, nh)
    b, q = c // QG, lax.rem(c, QG)
    d = z * QG + q
    core = lax.rem(c, 2)
    other = 1 - core
    sibling = c + 1 - 2 * core

    def remote(src, dst, phase, zz, cc):
        pltpu.make_async_remote_copy(
            src_ref=src, dst_ref=dst, send_sem=send.at[phase], recv_sem=recv.at[phase],
            device_id=(zz, cc), device_id_type=MESH,
        ).start()

    def here(src, dst, phase):
        pltpu.make_async_copy(src, dst, recv.at[phase]).start()

    def wait(ref, sems, phase):
        pltpu.make_async_copy(ref, ref, sems.at[phase]).wait()

    near = pl.ds(0, nc - 1)
    quarter = wb.at[0, pl.ds(0, nh)]
    small = a1s.at[pl.ds(0, ng - 1)]
    filters = gfr.at[pl.ds(0, ng - 1)]
    half = nz // 2
    brings = {
        0: a1r, 1: a2r, 2: a3r, 3: a4r, 4: quarter, 23: quarter, 5: cotg.at[:, 0], 6: quarter,
        7: midg.at[:, 0], 8: gmr, 9: prr, 10: gr1, 11: gfr, 12: gr2, 13: gfz,
        14: gfall.at[:, pl.ds(0, half)], 15: cotg.at[:, 0], 16: midg.at[:, 0],
        17: gmx, 18: prx, 21: quarter, 22: quarter, 24: quarter, 25: quarter, 6: quarter, 20: quarter,
    }
    brings[19] = brings[14]
    leaves = {
        0: small, 1: small, 2: small, 3: small, 5: cotg.at[near, 0], 6: quarter, 7: midg.at[near, 0],
        8: gmr.at[near], 9: prr.at[near], 10: gr1.at[near], 11: filters,
        12: gr2.at[pl.ds(0, nz - 1)], 13: gfz.at[pl.ds(0, nz - 1)], 14: gfall.at[near, pl.ds(0, half)], 15: brings[15], 16: brings[16],
        17: gmx, 18: prx, 19: brings[19], 21: quarter, 22: quarter, 20: quarter, 24: quarter, 25: quarter,
    }

    def arrived(phase):
        wait(brings[phase], recv, phase)

    def left(phase):
        if phase in leaves:
            wait(leaves[phase], send, phase)
        elif phase in (4, 23):

            @pl.when(h != z)
            def _():
                wait(wb.at[0, pl.ds(0, nz)], send, phase)

            @pl.when(h == z)
            def _():
                wait(wb.at[0, pl.ds(0, nz - 1)], send, phase)

    def each(low, high, body):
        def step(k, carry):
            body(k)
            return carry
        lax.fori_loop(low, high, step, 0)

    fetches = []
    for sources in (
        ((tokens_in, tokens),), ((plh_in, plh),), ((pll_in, pll),),
        ((up_in, wts.at[0]),), ((down_in, wts.at[1]),),
        ((cotangent_in, cotangent),), ((mg_in, mg),), ((mt_in, mt),), ((lane_in, lane),),
        ((row_in, row),), ((filter_in.at[:, b], fil.at[0]),), ((filter_out.at[:, b], fil.at[1]),),
    ):
        fetches.append(
            [pltpu.make_async_copy(src, dst, local.at[len(fetches)]) for src, dst in sources]
        )
        for fetch in fetches[-1]:
            fetch.start()

    barrier = pltpu.get_barrier_semaphore()

    def greet(zz, cc):
        pl.semaphore_signal(barrier, inc=1, device_id=(zz, cc), device_id_type=MESH)

    each(1, nc, lambda k: greet(z, lax.rem(c + k, nc)))
    each(0, (nz - 1) * QG, lambda k: greet(lax.rem(z + 1 + k // QG, nz), b * QG + lax.rem(k, QG)))
    each(1, nz, lambda k: greet(lax.rem(z + k, nz), y * nh + z))

    @pl.when(h != z)
    def _():
        each(0, nh, lambda k: greet(h, y * nh + k))

    for phase in (0, 1, 2, 3, 4):
        for fetch in fetches[phase]:
            fetch.wait()
    for i in range(planes):
        toks_t[i * width:(i + 1) * width] = tokens[:, i * plane:(i + 1) * plane]

    def group_out(src, dst, phase):
        def one(k):
            dd = lax.rem(d + STRIDE * k, ng)
            remote(src.at[dd], dst.at[q, z], phase, dd // QG, b * QG + lax.rem(dd, QG))
        each(1, ng, one)
        here(src.at[d], dst.at[q, z], phase)

    def group_back(src, dst, phase):
        def one(k):
            dd = lax.rem(d + STRIDE * k, ng)
            zz, qq = dd // QG, lax.rem(dd, QG)
            remote(src.at[qq, zz], dst.at[d], phase, zz, b * QG + qq)
        each(1, ng, one)
        here(src.at[q, z], dst.at[d], phase)

    def slab_planes(src, dst, phase):
        def one(k):
            cc = lax.rem(c + STRIDE * k, nc)
            part = lax.rem(cc, 2)
            remote(src.at[cc // nh, part], dst.at[c, part], phase, z, cc)
        each(1, nc, one)
        here(src.at[y, core], dst.at[c, core], phase)

    def share(ref, phase):
        remote(ref.at[:, core], ref.at[:, core], phase, z, sibling)

    def slab_parts(src, dst, phase):
        def one(k):
            cc = lax.rem(c + STRIDE * k, nc)
            remote(src.at[cc], dst.at[c], phase, z, cc)
        each(1, nc, one)
        here(src.at[c], dst.at[c], phase)

    def plane_out(parts, dst):
        out = None
        for table, values in parts:
            term = dot(table[...], values, 1, 1)
            out = term if out is None else out + term
        dst[...] = out.astype(bf16).reshape(dst.shape)

    def plane_back(src):
        values = src[...].reshape(ng * comps, LANES)
        return dot(values, plh[...], 0, 0) + dot(values, pll[...], 0, 0)

    first_group = jnp.logical_and(z == 0, q == 0)

    def edge_table():
        return jnp.where(first_group, mt[...], mg[...])

    def evaluate(src):
        rows = nz * comps
        wide = jnp.concatenate([src[k].reshape(rows, LANES) for k in range(QG)], axis=1)
        wide = dot(wide, lane[...]).astype(bf16)
        wide = dot(row[...], wide)
        step = 2 * nz
        lines = jnp.concatenate(
            [
                jnp.concatenate(
                    [wide[k * step:(k + 1) * step, i * LANES:(i + 1) * LANES] for i in range(planes)],
                    axis=0,
                )
                for k in range(cols)
            ],
            axis=1,
        )
        edge = 2 * LANES
        first = dot(edge_table(), lines[:, :edge], precision=HIGHEST)
        rest = dot(mg[...], lines[:, edge:], precision=HIGHEST)
        spec = jnp.concatenate([first, rest], axis=1)
        mids = 2 * nx
        return jnp.concatenate(
            [
                jnp.concatenate(
                    [spec[:mids, k * LANES:(k + 1) * LANES], spec[mids:, k * LANES:(k + 1) * LANES]],
                    axis=1,
                )
                for k in range(cols)
            ],
            axis=0,
        )

    def collect(values, dst):
        mids = 2 * nx
        spec = jnp.concatenate(
            [
                jnp.concatenate(
                    [values[k * mids:(k + 1) * mids, :LANES], values[k * mids:(k + 1) * mids, LANES:]],
                    axis=0,
                )
                for k in range(cols)
            ],
            axis=1,
        )
        edge = 2 * LANES
        first = dot(edge_table(), spec[:, :edge], 0, 0, precision=HIGHEST)
        rest = dot(mg[...], spec[:, edge:], 0, 0, precision=HIGHEST)
        lines = jnp.concatenate([first, rest], axis=1)
        step = 2 * nz
        wide = jnp.concatenate(
            [
                jnp.concatenate(
                    [lines[i * step:(i + 1) * step, k * LANES:(k + 1) * LANES] for i in range(planes)],
                    axis=1,
                )
                for k in range(cols)
            ],
            axis=0,
        ).astype(bf16)
        wide = dot(row[...], wide, 0, 0).astype(bf16)
        wide = dot(wide, lane[...], 1, 1).astype(bf16)
        for k in range(QG):
            dst[k] = wide[:, k * LANES:(k + 1) * LANES].reshape(nz, comps, LANES)

    plane_out([(plh, toks_t[...]), (pll, toks_t[...])], a1s)
    pl.semaphore_wait(
        barrier, nc - 1 + (nz - 1) * QG + nz - 1 + jnp.where(h != z, nh, 0)
    )
    group_out(a1s, a1r, 0)

    wcols = y * nh + z

    def spread(part):
        def one(k):
            zz = lax.rem(z + h + k, nz)
            same = jnp.logical_and(zz == z, h == z)

            @pl.when(jnp.logical_not(same))
            def _():
                remote(wts.at[part], wb.at[part, c], (4, 23)[part], zz, wcols)

            @pl.when(same)
            def _():
                here(wts.at[part], wb.at[part, c], (4, 23)[part])
        each(0, nz, one)

    spread(0)
    spread(1)
    for fetch in fetches[5]:
        fetch.wait()
    for i in range(planes):
        cts[i] = cotangent[:, i * plane:(i + 1) * plane].reshape(2, width // 2, plane)
    slab_planes(cts, cotg, 5)

    for phase in range(6, 12):
        for fetch in fetches[phase]:
            fetch.wait()

    def complex_matrix(k):
        real, imag = fil[k, 0], fil[k, 1]
        return jnp.concatenate(
            [jnp.concatenate([real, imag], axis=1), jnp.concatenate([-imag, real], axis=1)], axis=0
        )

    arrived(0)
    x = evaluate(a1r)
    xs[...] = x
    a = dot(x, complex_matrix(0), precision=HIGHEST)
    as_[...] = a
    collect(dot(gelu(a), complex_matrix(1), precision=HIGHEST), a2s)
    group_back(a2s, a2r, 1)

    after, before = lax.rem(y + 1, ny), lax.rem(y + ny - 1, ny)

    def around(part):
        arrived((4, 23)[part])
        rows = wb.at[part, pl.ds(y * nh, nh)]
        remote(rows, rows, (6, 20)[part], z, after * nh + h)
        remote(rows, rows, (21, 24)[part], z, before * nh + h)

    def onward(part):
        for k, phase, source, to in ((0, (6, 20)[part], before, after), (1, (21, 24)[part], after, before)):
            arrived(phase)
            rows = wb.at[part, pl.ds(source * nh + k * (nh // 2), nh // 2)]
            remote(rows, rows, (22, 25)[part], z, to * nh + h)

    around(0)
    arrived(5)
    share(cotg, 15)

    arrived(1)
    middle = (toks_t[...].astype(f32) + plane_back(a2r)).astype(bf16)
    mid[...] = middle.reshape(mid.shape)
    slab_planes(mid, midg, 7)
    around(1)
    onward(0)
    arrived(7)
    share(midg, 16)

    tile = min(LANES, hidden)
    chans = nc * width

    def hidden_tile(k):
        return pl.ds(pl.multiple_of(k * tile, tile), tile)

    onward(1)
    arrived(15)
    arrived(22)
    arrived(25)

    def back_step(k):
        s = hidden_tile(k)
        back[s, :] = dot(
            wb[1, :, :, s].reshape(chans, tile), cotg[...].reshape(chans, plane), 0, 0
        )
    each(0, hidden // tile, back_step)

    arrived(16)

    def pre_step(k):
        s = hidden_tile(k)
        pre = dot(wb[0, :, :, s].reshape(chans, tile), midg[...].reshape(chans, plane), 0, 0)
        hid[s, :] = gelu(pre).astype(bf16)
        gpre[s, :] = (back[s, :] * gelu_slope(pre)).astype(bf16)
    each(0, hidden // tile, pre_step)

    few = QG

    def shares(weights, values, parts, extra, phase):
        def one(k):
            s = pl.ds(k * few, few)
            part = dot(weights[s].reshape(few * width, hidden), values[...])
            parts[s] = part.astype(bf16).reshape(few, 2, width // 2, plane)
            remote(parts.at[s, other], extra.at[s], phase, z, sibling)
        each(0, nc // few, one)

    def add_pair(parts, extra, total, phase):
        arrived(phase)

        def one(k):
            s = pl.ds(k * few, few)
            total[s] = (parts[s, core].astype(f32) + extra[s].astype(f32)).astype(bf16)
        each(0, nc // few, one)

    def plane_sum(parts, i):
        halves = []
        for k in range(2):
            part = parts[i * nh + k].astype(f32)
            for j in range(k + 2, nh, 2):
                part = part + parts[i * nh + j].astype(f32)
            halves.append(part)
        return jnp.concatenate(halves, axis=0)

    shares(wb.at[0], gpre, gms, gmx, 17)

    def gw_step(k):
        s = pl.ds(k * few, few)
        part = dot(midg[s].reshape(few * width, plane), gpre[...], 1, 1)
        gw[s, 0] = part.astype(bf16).reshape(few, width, hidden)
        part = dot(cotg[s].reshape(few * width, plane), hid[...], 1, 1)
        gw[s, 1] = part.astype(bf16).reshape(few, width, hidden)
    each(0, nc // few, gw_step)

    add_pair(gms, gmx, gmh, 17)
    slab_parts(gmh, gmr, 8)
    shares(wb.at[1], hid, prs, prx, 18)

    arrived(8)
    gm = jnp.concatenate(
        [cts[i].reshape(width, plane).astype(f32) + plane_sum(gmr, i) for i in range(planes)], axis=0
    )
    high, low = split(gm)
    plane_out([(plh, high), (plh, low), (pll, high)], a3s)
    group_out(a3s, a3r, 2)

    add_pair(prs, prx, prh, 18)
    slab_parts(prh, prr, 9)
    slab_parts(gw, gr1, 10)

    arrived(2)
    dy = evaluate(a3r)
    a = as_[...]
    da = dot(dy, complex_matrix(1), 1, 1, precision=HIGHEST) * gelu_slope(a)

    def fold(g):
        return g[:LANES, :LANES] + g[LANES:, LANES:], g[:LANES, LANES:] - g[LANES:, :LANES]

    in_r, in_i = fold(dot(xs[...], da, 0, 0, precision=HIGHEST))
    out_r, out_i = fold(dot(gelu(a), dy, 0, 0, precision=HIGHEST))
    grads = jnp.concatenate([in_r, in_i, out_r, out_i], axis=0)
    gfs[...] = grads.astype(bf16).reshape(gfs.shape)

    group_back(gfs, gfr, 11)
    collect(dot(da, complex_matrix(0), 1, 1, precision=HIGHEST), a4s)
    group_back(a4s, a4r, 3)

    arrived(11)
    part = gfr[0].astype(f32)
    for k in range(1, ng):
        part = part + gfr[k].astype(f32)
    gfp[...] = part.astype(bf16)

    each(1, nz, lambda k: remote(gfp, gfz.at[z], 13, lax.rem(z + k, nz), c))
    here(gfp, gfz.at[z], 13)

    arrived(10)

    def gs_step(k):
        part = gr1[k].astype(f32)
        for i in range(1, ny):
            part = part + gr1[i * nh + k].astype(f32)
        gs[k] = part.astype(bf16)
    each(0, nh, gs_step)

    def gs_out(k):
        zz = lax.rem(z + k, nz)
        remote(gs.at[zz], gr2.at[z], 12, zz, c)
    each(1, nz, gs_out)
    here(gs.at[z], gr2.at[z], 12)

    arrived(13)

    def gf_slab(k):
        cc = lax.rem(c + STRIDE * k, nc)
        own = pl.ds(lax.rem(cc, 2) * half, half)
        remote(gfz.at[own], gfall.at[c, own], 14, z, cc)
    each(1, nc, gf_slab)
    here(gfz.at[pl.ds(core * half, half)], gfall.at[c, pl.ds(core * half, half)], 14)

    arrived(3)
    whole = (gm + plane_back(a4r)).astype(bf16)
    for i in range(planes):
        gtok[:, i * plane:(i + 1) * plane] = whole[i * width:(i + 1) * width]

    arrived(14)
    own = gfall.at[:, pl.ds(core * half, half)]
    remote(own, own, 19, z, sibling)

    arrived(9)
    for i in range(planes):
        whole = mid[i].reshape(width, plane).astype(f32) + plane_sum(prr, i)
        mixed[:, i * plane:(i + 1) * plane] = whole.astype(bf16)

    arrived(12)
    for k, dst in ((0, gup), (1, gdn)):
        part = gr2[0, k].astype(f32)
        for i in range(1, nz):
            part = part + gr2[i, k].astype(f32)
        dst[...] = part

    arrived(19)
    for k in range(nb):
        for j in range(QG):
            (gfi, gfo)[j // 2][j % 2, k] = gfall[k * QG + j].astype(f32).reshape(LANES, LANES)

    for phase in range(26):
        left(phase)


def solution(mesh):
    nz, nc = mesh.shape["tok"], mesh.shape["ch"]

    def local(tokens, filter_in, filter_out, up_weight, down_weight, cotangent):
        rows, width = tokens.shape
        plane = NY * NZ
        planes = rows // plane
        ng = nz * QG
        nb = nc // QG
        nh = nc // planes
        nx = nz * planes
        hidden = up_weight.shape[1]
        comps = plane // ng
        assert nh == nz and planes * width == LANES and QG * width == LANES
        tabs = tables(nz, planes)
        evals = comps // 2 * 2 * nx
        fr = 4 * LANES // ng
        halves = (nc, width // 2, plane)
        block = (nc, 2, width // 2, plane)
        out_shape = (ng, comps, LANES)
        back_shape = (QG, nz, comps, LANES)
        scratch = [
            pltpu.VMEM(shape, bf16)
            for shape in (out_shape, back_shape, back_shape, out_shape) * 2
        ] + [
            pltpu.VMEM((evals, 2 * LANES), f32),
            pltpu.VMEM((evals, 2 * LANES), f32),
            pltpu.VMEM((2, 2, LANES, LANES), f32),
            pltpu.VMEM((LANES, plane), bf16),
            pltpu.VMEM((planes, 2, width // 2, plane), bf16),
            pltpu.VMEM((2, width, hidden), bf16),
            pltpu.VMEM((planes, 2, width // 2, plane), bf16),
            pltpu.VMEM(block, bf16),
            pltpu.VMEM(block, bf16),
            pltpu.VMEM((2, nc, width, hidden), bf16),
            pltpu.VMEM((hidden, plane), f32),
            pltpu.VMEM((hidden, plane), bf16),
            pltpu.VMEM((hidden, plane), bf16),
        ] + [
            pltpu.VMEM(shape, bf16) for shape in (block, halves, halves, halves) * 2
        ] + [
            pltpu.VMEM((nc, 2, width, hidden), bf16),
            pltpu.VMEM((nc, 2, width, hidden), bf16),
            pltpu.VMEM((nh, 2, width, hidden), bf16),
            pltpu.VMEM((nz, 2, width, hidden), bf16),
            pltpu.VMEM((QG, nz, fr, LANES), bf16),
            pltpu.VMEM((ng, fr, LANES), bf16),
            pltpu.VMEM((fr, LANES), bf16),
            pltpu.VMEM((nz, fr, LANES), bf16),
            pltpu.VMEM((nc, nz, fr, LANES), bf16),
            pltpu.VMEM((width, rows), bf16),
            pltpu.VMEM((width, rows), bf16),
            pltpu.VMEM((plane, plane), bf16),
            pltpu.VMEM((plane, plane), bf16),
            pltpu.VMEM((4 * nx, 2 * nx), f32),
            pltpu.VMEM((4 * nx, 2 * nx), f32),
            pltpu.VMEM((QG * LANES, QG * LANES), bf16),
            pltpu.VMEM((nz * comps, nz * comps), bf16),
            pltpu.SemaphoreType.DMA((26,)),
            pltpu.SemaphoreType.DMA((26,)),
            pltpu.SemaphoreType.DMA((12,)),
        ]
        vmem = pl.BlockSpec(memory_space=pltpu.VMEM)
        anywhere = pl.BlockSpec(memory_space=pl.ANY)
        flops = 12 * plane * hidden * nc * width
        mixed, gtok, gup, gdn, gfi, gfo = pl.pallas_call(
            functools.partial(kernel, nz, nc, planes),
            out_shape=(
                jax.ShapeDtypeStruct((width, rows), bf16),
                jax.ShapeDtypeStruct((width, rows), bf16),
                jax.ShapeDtypeStruct((width, hidden), f32),
                jax.ShapeDtypeStruct((width, hidden), f32),
                jax.ShapeDtypeStruct(filter_in.shape, f32),
                jax.ShapeDtypeStruct(filter_out.shape, f32),
            ),
            in_specs=[anywhere] * 12,
            out_specs=[vmem] * 6,
            scratch_shapes=scratch,
            compiler_params=pltpu.CompilerParams(
                collective_id=0, has_side_effects=True, vmem_limit_bytes=60 * 2**20
            ),
            cost_estimate=pl.CostEstimate(flops=flops, bytes_accessed=2**24, transcendentals=2**20),
        )(
            tokens.T, cotangent.T, up_weight, down_weight.T, filter_in, filter_out,
            tabs["high"], tabs["low"], tabs["pair"], tabs["two"], tabs["lane"], tabs["row"],
        )

        return mixed.T, gtok.T, gup, gdn.T, gfi, gfo

    in_specs = (P("tok", "ch"), P(), P(), P("ch", "tok"), P("tok", "ch"), P("tok", "ch"))
    out_specs = (P("tok", "ch"), P("tok", "ch"), P("ch", "tok"), P("tok", "ch"), P(), P())
    return jax.shard_map(local, mesh=mesh, in_specs=in_specs, out_specs=out_specs, check_vma=False)
```

```python
import functools
import math

import jax
import jax.numpy as jnp
import ml_dtypes
import numpy as np
from jax import lax
from jax.experimental import pallas as pl
from jax.experimental.pallas import tpu as pltpu
from jax.sharding import PartitionSpec as P

NY = 64
NZ = 8
QG = 4
STRIDE = 11
LANES = 128

f32 = jnp.float32
bf16 = jnp.bfloat16
HIGHEST = lax.Precision.HIGHEST
MESH = pl.DeviceIdType.MESH


@functools.lru_cache(None)
def tables(nz, planes):
    groups = nz * QG
    nx = nz * planes
    plane = NY * NZ
    singles = [(0, 0), (0, NZ // 2), (NY // 2, 0), (NY // 2, NZ // 2)]
    pairs = []
    for v in range(NY):
        for w in range(NZ):
            other = ((-v) % NY, (-w) % NZ)
            if (v, w) < other:
                pairs.append((v, w))
    j = np.repeat(np.arange(NY), NZ)
    k = np.tile(np.arange(NZ), NY)
    rows = []
    for v, w in singles:
        rows.append(np.cos(2 * np.pi * (v * j / NY + w * k / NZ)))
    for v, w in pairs:
        angle = 2 * np.pi * (((v * j) % NY) / NY + ((w * k) % NZ) / NZ)
        rows.append(np.cos(angle))
        rows.append(-np.sin(angle))
    full = np.stack(rows) / math.sqrt(plane)
    assert full.shape == (plane, plane)
    high = full.astype(ml_dtypes.bfloat16)
    low = (full - high.astype(np.float64)).astype(ml_dtypes.bfloat16)
    u = np.arange(nx)
    turn = 2 * np.pi * ((u[:, None] * u[None, :]) % nx) / nx
    cos, sin = np.cos(turn) / math.sqrt(nx), np.sin(turn) / math.sqrt(nx)
    pair = np.zeros((2, nx, 2, 2, nx))
    pair[0, :, 0, 0], pair[0, :, 0, 1] = cos, sin
    pair[1, :, 0, 0], pair[1, :, 0, 1] = -sin, cos
    pair[0, :, 1, 0], pair[0, :, 1, 1] = cos, sin
    pair[1, :, 1, 0], pair[1, :, 1, 1] = sin, -cos
    two = np.zeros((2, nx, 2, 2, nx))
    two[0, :, 0, 0], two[1, :, 0, 0] = cos, -sin
    two[0, :, 1, 1], two[1, :, 1, 1] = cos, -sin

    def ordered(table):
        table = table.reshape(4 * nx, 2, nz, planes).transpose(0, 3, 1, 2)
        return table.reshape(4 * nx, 2 * nx).astype(np.float32)

    width = LANES // QG
    lane = np.zeros((QG * LANES, QG * LANES), np.float32)
    for q in range(QG):
        for i in range(planes):
            for c in range(width):
                lane[q * LANES + i * width + c, i * LANES + q * width + c] = 1.0
    comps = plane // groups
    row = np.zeros((nz * comps, nz * comps), np.float32)
    for z in range(nz):
        for r in range(comps):
            row[r * nz + z, z * comps + r] = 1.0
    return dict(
        high=high,
        low=low,
        pair=ordered(pair),
        two=ordered(two),
        lane=lane.astype(ml_dtypes.bfloat16),
        row=row.astype(ml_dtypes.bfloat16),
    )


def dot(a, b, ca=1, cb=0, precision=None):
    return lax.dot_general(
        a, b, (((ca,), (cb,)), ((), ())), precision=precision, preferred_element_type=f32
    )


def split(x):
    high = x.astype(bf16)
    return high, (x - high.astype(f32)).astype(bf16)


def dot3(a, b, ca=1, cb=0):
    (ah, al), (bh, bl) = split(a), split(b)
    return dot(ah, bh, ca, cb) + (dot(ah, bl, ca, cb) + dot(al, bh, ca, cb))


SCALE = math.sqrt(2.0 / math.pi)
CUBIC = 0.044715


def gelu(x):
    t = jnp.tanh(SCALE * (x + CUBIC * (x * x * x)))
    return 0.5 * x * (1.0 + t)


def gelu_slope(x):
    t = jnp.tanh(SCALE * (x + CUBIC * (x * x * x)))
    return 0.5 * (1.0 + t) + 0.5 * x * (1.0 - t * t) * (SCALE * (1.0 + 3.0 * CUBIC * (x * x)))


def kernel(
    nz, nc, planes,
    tokens_in, cotangent_in, up_in, down_in, filter_in, filter_out,
    plh_in, pll_in, mg_in, mt_in, lane_in, row_in,
    mixed, gtok, gup, gdn, gfi, gfo,
    a1s, a1r, a2s, a2r, a3s, a3r, a4s, a4r,
    xs, as_, fil, toks_t, cts, wts,
    mid, midg, cotg, wb, back, hid, gpre,
    gms, gmx, gmh, gmr, prs, prx, prh, prr, gw, gr1, gs, gr2,
    gfs, gfr, gfp, gfz, gfall,
    tokens, cotangent, plh, pll, mg, mt, lane, row,
    send, recv, local,
):
    ny = planes
    nh = nc // ny
    ng = nz * QG
    nb = nc // QG
    nx = nz * planes
    comps = a1s.shape[1]
    cols = comps // 2
    width, plane = wts.shape[1], mid.shape[3]
    hidden = hid.shape[0]
    z = lax.axis_index("tok")
    c = lax.axis_index("ch")
    y, h = c // nh, lax.rem(c, nh)
    b, q = c // QG, lax.rem(c, QG)
    d = z * QG + q
    core = lax.rem(c, 2)
    other = 1 - core
    sibling = c + 1 - 2 * core

    def remote(src, dst, phase, zz, cc):
        pltpu.make_async_remote_copy(
            src_ref=src, dst_ref=dst, send_sem=send.at[phase], recv_sem=recv.at[phase],
            device_id=(zz, cc), device_id_type=MESH,
        ).start()

    def here(src, dst, phase):
        pltpu.make_async_copy(src, dst, recv.at[phase]).start()

    def wait(ref, sems, phase):
        pltpu.make_async_copy(ref, ref, sems.at[phase]).wait()

    near = pl.ds(0, nc - 1)
    quarter = wb.at[0, pl.ds(0, nh)]
    small = a1s.at[pl.ds(0, ng - 1)]
    filters = gfr.at[pl.ds(0, ng - 1)]
    half = nz // 2
    brings = {
        0: a1r, 1: a2r, 2: a3r, 3: a4r, 4: quarter, 23: quarter, 5: cotg.at[:, 0], 6: quarter,
        7: midg.at[:, 0], 8: gmr, 9: prr, 10: gr1.at[0], 26: gr1.at[0], 11: gfr, 12: gr2.at[0], 27: gr2.at[0], 13: gfz,
        14: gfall.at[:, pl.ds(0, half)], 15: cotg.at[:, 0], 16: midg.at[:, 0],
        17: gmx, 18: prx, 21: quarter, 22: quarter, 24: quarter, 25: quarter, 6: quarter, 20: quarter,
    }
    brings[19] = brings[14]
    leaves = {
        0: small, 1: small, 2: small, 3: small, 5: cotg.at[near, 0], 6: quarter, 7: midg.at[near, 0],
        8: gmr.at[near], 9: prr.at[near], 10: gr1.at[0, near], 26: gr1.at[0, near], 11: filters,
        12: gr2.at[0, pl.ds(0, nz - 1)], 27: gr2.at[0, pl.ds(0, nz - 1)], 13: gfz.at[pl.ds(0, nz - 1)], 14: gfall.at[near, pl.ds(0, half)], 15: brings[15], 16: brings[16],
        17: gmx, 18: prx, 19: brings[19], 21: quarter, 22: quarter, 20: quarter, 24: quarter, 25: quarter,
    }

    def arrived(phase):
        wait(brings[phase], recv, phase)

    def left(phase):
        if phase in leaves:
            wait(leaves[phase], send, phase)
        elif phase in (4, 23):

            @pl.when(h != z)
            def _():
                wait(wb.at[0, pl.ds(0, nz)], send, phase)

            @pl.when(h == z)
            def _():
                wait(wb.at[0, pl.ds(0, nz - 1)], send, phase)

    def each(low, high, body):
        def step(k, carry):
            body(k)
            return carry
        lax.fori_loop(low, high, step, 0)

    fetches = []
    for sources in (
        ((tokens_in, tokens),), ((plh_in, plh),), ((pll_in, pll),),
        ((up_in, wts.at[0]),), ((down_in, wts.at[1]),),
        ((cotangent_in, cotangent),), ((mg_in, mg),), ((mt_in, mt),), ((lane_in, lane),),
        ((row_in, row),), ((filter_in.at[:, b], fil.at[0]),), ((filter_out.at[:, b], fil.at[1]),),
    ):
        fetches.append(
            [pltpu.make_async_copy(src, dst, local.at[len(fetches)]) for src, dst in sources]
        )
        for fetch in fetches[-1]:
            fetch.start()

    barrier = pltpu.get_barrier_semaphore()

    def greet(zz, cc):
        pl.semaphore_signal(barrier, inc=1, device_id=(zz, cc), device_id_type=MESH)

    each(1, nc, lambda k: greet(z, lax.rem(c + k, nc)))
    each(0, (nz - 1) * QG, lambda k: greet(lax.rem(z + 1 + k // QG, nz), b * QG + lax.rem(k, QG)))
    each(1, nz, lambda k: greet(lax.rem(z + k, nz), y * nh + z))

    @pl.when(h != z)
    def _():
        each(0, nh, lambda k: greet(h, y * nh + k))

    for phase in (0, 1, 2, 3, 4):
        for fetch in fetches[phase]:
            fetch.wait()
    for i in range(planes):
        toks_t[i * width:(i + 1) * width] = tokens[:, i * plane:(i + 1) * plane]

    def group_out(src, dst, phase):
        def one(k):
            dd = lax.rem(d + STRIDE * k, ng)
            remote(src.at[dd], dst.at[q, z], phase, dd // QG, b * QG + lax.rem(dd, QG))
        each(1, ng, one)
        here(src.at[d], dst.at[q, z], phase)

    def group_back(src, dst, phase):
        def one(k):
            dd = lax.rem(d + STRIDE * k, ng)
            zz, qq = dd // QG, lax.rem(dd, QG)
            remote(src.at[qq, zz], dst.at[d], phase, zz, b * QG + qq)
        each(1, ng, one)
        here(src.at[q, z], dst.at[d], phase)

    def slab_planes(src, dst, phase):
        def one(k):
            cc = lax.rem(c + STRIDE * k, nc)
            part = lax.rem(cc, 2)
            remote(src.at[cc // nh, part], dst.at[c, part], phase, z, cc)
        each(1, nc, one)
        here(src.at[y, core], dst.at[c, core], phase)

    def share(ref, phase):
        remote(ref.at[:, core], ref.at[:, core], phase, z, sibling)

    def slab_parts(src, dst, phase):
        def one(k):
            cc = lax.rem(c + STRIDE * k, nc)
            remote(src.at[cc], dst.at[c], phase, z, cc)
        each(1, nc, one)
        here(src.at[c], dst.at[c], phase)

    def plane_out(parts, dst):
        out = None
        for table, values in parts:
            term = dot(table[...], values, 1, 1)
            out = term if out is None else out + term
        dst[...] = out.astype(bf16).reshape(dst.shape)

    def plane_back(src):
        values = src[...].reshape(ng * comps, LANES)
        return dot(values, plh[...], 0, 0) + dot(values, pll[...], 0, 0)

    first_group = jnp.logical_and(z == 0, q == 0)

    def edge_table():
        return jnp.where(first_group, mt[...], mg[...])

    def evaluate(src):
        rows = nz * comps
        wide = jnp.concatenate([src[k].reshape(rows, LANES) for k in range(QG)], axis=1)
        wide = dot(wide, lane[...]).astype(bf16)
        wide = dot(row[...], wide)
        step = 2 * nz
        lines = jnp.concatenate(
            [
                jnp.concatenate(
                    [wide[k * step:(k + 1) * step, i * LANES:(i + 1) * LANES] for i in range(planes)],
                    axis=0,
                )
                for k in range(cols)
            ],
            axis=1,
        )
        edge = 2 * LANES
        first = dot(edge_table(), lines[:, :edge], precision=HIGHEST)
        rest = dot(mg[...], lines[:, edge:], precision=HIGHEST)
        spec = jnp.concatenate([first, rest], axis=1)
        mids = 2 * nx
        return jnp.concatenate(
            [
                jnp.concatenate(
                    [spec[:mids, k * LANES:(k + 1) * LANES], spec[mids:, k * LANES:(k + 1) * LANES]],
                    axis=1,
                )
                for k in range(cols)
            ],
            axis=0,
        )

    def collect(values, dst):
        mids = 2 * nx
        spec = jnp.concatenate(
            [
                jnp.concatenate(
                    [values[k * mids:(k + 1) * mids, :LANES], values[k * mids:(k + 1) * mids, LANES:]],
                    axis=0,
                )
                for k in range(cols)
            ],
            axis=1,
        )
        edge = 2 * LANES
        first = dot(edge_table(), spec[:, :edge], 0, 0, precision=HIGHEST)
        rest = dot(mg[...], spec[:, edge:], 0, 0, precision=HIGHEST)
        lines = jnp.concatenate([first, rest], axis=1)
        step = 2 * nz
        wide = jnp.concatenate(
            [
                jnp.concatenate(
                    [lines[i * step:(i + 1) * step, k * LANES:(k + 1) * LANES] for i in range(planes)],
                    axis=1,
                )
                for k in range(cols)
            ],
            axis=0,
        ).astype(bf16)
        wide = dot(row[...], wide, 0, 0).astype(bf16)
        wide = dot(wide, lane[...], 1, 1).astype(bf16)
        for k in range(QG):
            dst[k] = wide[:, k * LANES:(k + 1) * LANES].reshape(nz, comps, LANES)

    plane_out([(plh, toks_t[...]), (pll, toks_t[...])], a1s)
    pl.semaphore_wait(
        barrier, nc - 1 + (nz - 1) * QG + nz - 1 + jnp.where(h != z, nh, 0)
    )
    group_out(a1s, a1r, 0)

    wcols = y * nh + z

    def spread(part):
        def one(k):
            zz = lax.rem(z + h + k, nz)
            same = jnp.logical_and(zz == z, h == z)

            @pl.when(jnp.logical_not(same))
            def _():
                remote(wts.at[part], wb.at[part, c], (4, 23)[part], zz, wcols)

            @pl.when(same)
            def _():
                here(wts.at[part], wb.at[part, c], (4, 23)[part])
        each(0, nz, one)

    spread(0)
    spread(1)
    for fetch in fetches[5]:
        fetch.wait()
    for i in range(planes):
        cts[i] = cotangent[:, i * plane:(i + 1) * plane].reshape(2, width // 2, plane)
    slab_planes(cts, cotg, 5)

    for phase in range(6, 12):
        for fetch in fetches[phase]:
            fetch.wait()

    def complex_matrix(k):
        real, imag = fil[k, 0], fil[k, 1]
        return jnp.concatenate(
            [jnp.concatenate([real, imag], axis=1), jnp.concatenate([-imag, real], axis=1)], axis=0
        )

    arrived(0)
    x = evaluate(a1r)
    xs[...] = x
    a = dot3(x, complex_matrix(0))
    as_[...] = a
    collect(dot3(gelu(a), complex_matrix(1)), a2s)
    group_back(a2s, a2r, 1)

    after, before = lax.rem(y + 1, ny), lax.rem(y + ny - 1, ny)

    def around(part):
        arrived((4, 23)[part])
        rows = wb.at[part, pl.ds(y * nh, nh)]
        remote(rows, rows, (6, 20)[part], z, after * nh + h)
        remote(rows, rows, (21, 24)[part], z, before * nh + h)

    def onward(part):
        for k, phase, source, to in ((0, (6, 20)[part], before, after), (1, (21, 24)[part], after, before)):
            arrived(phase)
            rows = wb.at[part, pl.ds(source * nh + k * (nh // 2), nh // 2)]
            remote(rows, rows, (22, 25)[part], z, to * nh + h)

    around(0)
    arrived(5)
    share(cotg, 15)

    arrived(1)
    middle = (toks_t[...].astype(f32) + plane_back(a2r)).astype(bf16)
    mid[...] = middle.reshape(mid.shape)
    slab_planes(mid, midg, 7)
    around(1)
    onward(0)
    arrived(7)
    share(midg, 16)

    tile = min(LANES, hidden)
    chans = nc * width

    def hidden_tile(k):
        return pl.ds(pl.multiple_of(k * tile, tile), tile)

    onward(1)
    arrived(15)
    arrived(22)
    arrived(25)

    def back_step(k):
        s = hidden_tile(k)
        back[s, :] = dot(
            wb[1, :, :, s].reshape(chans, tile), cotg[...].reshape(chans, plane), 0, 0
        )
    each(0, hidden // tile, back_step)

    arrived(16)

    def pre_step(k):
        s = hidden_tile(k)
        pre = dot(wb[0, :, :, s].reshape(chans, tile), midg[...].reshape(chans, plane), 0, 0)
        hid[s, :] = gelu(pre).astype(bf16)
        gpre[s, :] = (back[s, :] * gelu_slope(pre)).astype(bf16)
    each(0, hidden // tile, pre_step)

    few = QG

    def shares(weights, values, parts, extra, phase):
        def one(k):
            s = pl.ds(k * few, few)
            part = dot(weights[s].reshape(few * width, hidden), values[...])
            parts[s] = part.astype(bf16).reshape(few, 2, width // 2, plane)
            remote(parts.at[s, other], extra.at[s], phase, z, sibling)
        each(0, nc // few, one)

    def add_pair(parts, extra, total, phase):
        arrived(phase)

        def one(k):
            s = pl.ds(k * few, few)
            total[s] = (parts[s, core].astype(f32) + extra[s].astype(f32)).astype(bf16)
        each(0, nc // few, one)

    def plane_sum(parts, i):
        halves = []
        for k in range(2):
            part = parts[i * nh + k].astype(f32)
            for j in range(k + 2, nh, 2):
                part = part + parts[i * nh + j].astype(f32)
            halves.append(part)
        return jnp.concatenate(halves, axis=0)

    shares(wb.at[0], gpre, gms, gmx, 17)

    def gw_step(k):
        s = pl.ds(k * few, few)
        part = dot(midg[s].reshape(few * width, plane), gpre[...], 1, 1)
        gw[0, s] = part.astype(bf16).reshape(few, width, hidden)
        part = dot(cotg[s].reshape(few * width, plane), hid[...], 1, 1)
        gw[1, s] = part.astype(bf16).reshape(few, width, hidden)
    each(0, nc // few, gw_step)

    add_pair(gms, gmx, gmh, 17)
    slab_parts(gmh, gmr, 8)
    slab_parts(gw.at[0], gr1.at[0], 10)
    shares(wb.at[1], hid, prs, prx, 18)

    def weight_sums(part):
        arrived((10, 26)[part])

        def one(k):
            total = gr1[part, k].astype(f32)
            for i in range(1, ny):
                total = total + gr1[part, i * nh + k].astype(f32)
            gs[part, k] = total.astype(bf16)
        each(0, nh, one)

        def out(k):
            zz = lax.rem(z + k, nz)
            remote(gs.at[part, zz], gr2.at[part, z], (12, 27)[part], zz, c)
        each(1, nz, out)
        here(gs.at[part, z], gr2.at[part, z], (12, 27)[part])

    arrived(8)
    gm = jnp.concatenate(
        [cts[i].reshape(width, plane).astype(f32) + plane_sum(gmr, i) for i in range(planes)], axis=0
    )
    high, low = split(gm)
    plane_out([(plh, high), (plh, low), (pll, high)], a3s)
    group_out(a3s, a3r, 2)

    slab_parts(gw.at[1], gr1.at[1], 26)

    arrived(2)
    dy = evaluate(a3r)
    a = as_[...]
    da = dot3(dy, complex_matrix(1), 1, 1) * gelu_slope(a)

    def fold(g):
        return g[:LANES, :LANES] + g[LANES:, LANES:], g[:LANES, LANES:] - g[LANES:, :LANES]

    in_r, in_i = fold(dot3(xs[...], da, 0, 0))
    out_r, out_i = fold(dot3(gelu(a), dy, 0, 0))
    grads = jnp.concatenate([in_r, in_i, out_r, out_i], axis=0)
    gfs[...] = grads.astype(bf16).reshape(gfs.shape)

    group_back(gfs, gfr, 11)
    collect(dot3(da, complex_matrix(0), 1, 1), a4s)
    group_back(a4s, a4r, 3)
    weight_sums(0)
    add_pair(prs, prx, prh, 18)
    slab_parts(prh, prr, 9)

    arrived(11)
    part = gfr[0].astype(f32)
    for k in range(1, ng):
        part = part + gfr[k].astype(f32)
    gfp[...] = part.astype(bf16)

    each(1, nz, lambda k: remote(gfp, gfz.at[z], 13, lax.rem(z + k, nz), c))
    here(gfp, gfz.at[z], 13)

    weight_sums(1)

    arrived(13)

    def gf_slab(k):
        cc = lax.rem(c + STRIDE * k, nc)
        own = pl.ds(lax.rem(cc, 2) * half, half)
        remote(gfz.at[own], gfall.at[c, own], 14, z, cc)
    each(1, nc, gf_slab)
    here(gfz.at[pl.ds(core * half, half)], gfall.at[c, pl.ds(core * half, half)], 14)

    arrived(3)
    whole = (gm + plane_back(a4r)).astype(bf16)
    for i in range(planes):
        gtok[:, i * plane:(i + 1) * plane] = whole[i * width:(i + 1) * width]

    arrived(14)
    own = gfall.at[:, pl.ds(core * half, half)]
    remote(own, own, 19, z, sibling)

    arrived(9)
    for i in range(planes):
        whole = mid[i].reshape(width, plane).astype(f32) + plane_sum(prr, i)
        mixed[:, i * plane:(i + 1) * plane] = whole.astype(bf16)

    for k, dst in ((0, gup), (1, gdn)):
        arrived((12, 27)[k])
        part = gr2[k, 0].astype(f32)
        for i in range(1, nz):
            part = part + gr2[k, i].astype(f32)
        dst[...] = part

    arrived(19)
    for k in range(nb):
        for j in range(QG):
            (gfi, gfo)[j // 2][j % 2, k] = gfall[k * QG + j].astype(f32).reshape(LANES, LANES)

    for phase in range(28):
        left(phase)


def solution(mesh):
    nz, nc = mesh.shape["tok"], mesh.shape["ch"]

    def local(tokens, filter_in, filter_out, up_weight, down_weight, cotangent):
        rows, width = tokens.shape
        plane = NY * NZ
        planes = rows // plane
        ng = nz * QG
        nb = nc // QG
        nh = nc // planes
        nx = nz * planes
        hidden = up_weight.shape[1]
        comps = plane // ng
        assert nh == nz and planes * width == LANES and QG * width == LANES
        tabs = tables(nz, planes)
        evals = comps // 2 * 2 * nx
        fr = 4 * LANES // ng
        halves = (nc, width // 2, plane)
        block = (nc, 2, width // 2, plane)
        out_shape = (ng, comps, LANES)
        back_shape = (QG, nz, comps, LANES)
        scratch = [
            pltpu.VMEM(shape, bf16)
            for shape in (out_shape, back_shape, back_shape, out_shape) * 2
        ] + [
            pltpu.VMEM((evals, 2 * LANES), f32),
            pltpu.VMEM((evals, 2 * LANES), f32),
            pltpu.VMEM((2, 2, LANES, LANES), f32),
            pltpu.VMEM((LANES, plane), bf16),
            pltpu.VMEM((planes, 2, width // 2, plane), bf16),
            pltpu.VMEM((2, width, hidden), bf16),
            pltpu.VMEM((planes, 2, width // 2, plane), bf16),
            pltpu.VMEM(block, bf16),
            pltpu.VMEM(block, bf16),
            pltpu.VMEM((2, nc, width, hidden), bf16),
            pltpu.VMEM((hidden, plane), f32),
            pltpu.VMEM((hidden, plane), bf16),
            pltpu.VMEM((hidden, plane), bf16),
        ] + [
            pltpu.VMEM(shape, bf16) for shape in (block, halves, halves, halves) * 2
        ] + [
            pltpu.VMEM((2, nc, width, hidden), bf16),
            pltpu.VMEM((2, nc, width, hidden), bf16),
            pltpu.VMEM((2, nh, width, hidden), bf16),
            pltpu.VMEM((2, nz, width, hidden), bf16),
            pltpu.VMEM((QG, nz, fr, LANES), bf16),
            pltpu.VMEM((ng, fr, LANES), bf16),
            pltpu.VMEM((fr, LANES), bf16),
            pltpu.VMEM((nz, fr, LANES), bf16),
            pltpu.VMEM((nc, nz, fr, LANES), bf16),
            pltpu.VMEM((width, rows), bf16),
            pltpu.VMEM((width, rows), bf16),
            pltpu.VMEM((plane, plane), bf16),
            pltpu.VMEM((plane, plane), bf16),
            pltpu.VMEM((4 * nx, 2 * nx), f32),
            pltpu.VMEM((4 * nx, 2 * nx), f32),
            pltpu.VMEM((QG * LANES, QG * LANES), bf16),
            pltpu.VMEM((nz * comps, nz * comps), bf16),
            pltpu.SemaphoreType.DMA((28,)),
            pltpu.SemaphoreType.DMA((28,)),
            pltpu.SemaphoreType.DMA((12,)),
        ]
        vmem = pl.BlockSpec(memory_space=pltpu.VMEM)
        anywhere = pl.BlockSpec(memory_space=pl.ANY)
        flops = 12 * plane * hidden * nc * width
        mixed, gtok, gup, gdn, gfi, gfo = pl.pallas_call(
            functools.partial(kernel, nz, nc, planes),
            out_shape=(
                jax.ShapeDtypeStruct((width, rows), bf16),
                jax.ShapeDtypeStruct((width, rows), bf16),
                jax.ShapeDtypeStruct((width, hidden), f32),
                jax.ShapeDtypeStruct((width, hidden), f32),
                jax.ShapeDtypeStruct(filter_in.shape, f32),
                jax.ShapeDtypeStruct(filter_out.shape, f32),
            ),
            in_specs=[anywhere] * 12,
            out_specs=[vmem] * 6,
            scratch_shapes=scratch,
            compiler_params=pltpu.CompilerParams(
                collective_id=0, has_side_effects=True, vmem_limit_bytes=60 * 2**20
            ),
            cost_estimate=pl.CostEstimate(flops=flops, bytes_accessed=2**24, transcendentals=2**20),
        )(
            tokens.T, cotangent.T, up_weight, down_weight.T, filter_in, filter_out,
            tabs["high"], tabs["low"], tabs["pair"], tabs["two"], tabs["lane"], tabs["row"],
        )

        return mixed.T, gtok.T, gup, gdn.T, gfi, gfo

    in_specs = (P("tok", "ch"), P(), P(), P("ch", "tok"), P("tok", "ch"), P("tok", "ch"))
    out_specs = (P("tok", "ch"), P("tok", "ch"), P("ch", "tok"), P("tok", "ch"), P(), P())
    return jax.shard_map(local, mesh=mesh, in_specs=in_specs, out_specs=out_specs, check_vma=False)
```

```python
import functools
import math

import jax
import jax.numpy as jnp
import ml_dtypes
import numpy as np
from jax import lax
from jax.experimental import pallas as pl
from jax.experimental.pallas import tpu as pltpu
from jax.sharding import PartitionSpec as P

NY = 64
NZ = 8
QG = 4
STRIDE = 11
LANES = 128

f32 = jnp.float32
bf16 = jnp.bfloat16
HIGHEST = lax.Precision.HIGHEST
MESH = pl.DeviceIdType.MESH


@functools.lru_cache(None)
def tables(nz, planes):
    groups = nz * QG
    nx = nz * planes
    plane = NY * NZ
    singles = [(0, 0), (0, NZ // 2), (NY // 2, 0), (NY // 2, NZ // 2)]
    pairs = []
    for v in range(NY):
        for w in range(NZ):
            other = ((-v) % NY, (-w) % NZ)
            if (v, w) < other:
                pairs.append((v, w))
    j = np.repeat(np.arange(NY), NZ)
    k = np.tile(np.arange(NZ), NY)
    rows = []
    for v, w in singles:
        rows.append(np.cos(2 * np.pi * (v * j / NY + w * k / NZ)))
    for v, w in pairs:
        angle = 2 * np.pi * (((v * j) % NY) / NY + ((w * k) % NZ) / NZ)
        rows.append(np.cos(angle))
        rows.append(-np.sin(angle))
    full = np.stack(rows) / math.sqrt(plane)
    assert full.shape == (plane, plane)
    high = full.astype(ml_dtypes.bfloat16)
    low = (full - high.astype(np.float64)).astype(ml_dtypes.bfloat16)
    u = np.arange(nx)
    turn = 2 * np.pi * ((u[:, None] * u[None, :]) % nx) / nx
    cos, sin = np.cos(turn) / math.sqrt(nx), np.sin(turn) / math.sqrt(nx)
    pair = np.zeros((2, nx, 2, 2, nx))
    pair[0, :, 0, 0], pair[0, :, 0, 1] = cos, sin
    pair[1, :, 0, 0], pair[1, :, 0, 1] = -sin, cos
    pair[0, :, 1, 0], pair[0, :, 1, 1] = cos, sin
    pair[1, :, 1, 0], pair[1, :, 1, 1] = sin, -cos
    two = np.zeros((2, nx, 2, 2, nx))
    two[0, :, 0, 0], two[1, :, 0, 0] = cos, -sin
    two[0, :, 1, 1], two[1, :, 1, 1] = cos, -sin

    def ordered(table):
        table = table.reshape(4 * nx, 2, nz, planes).transpose(0, 3, 1, 2)
        return table.reshape(4 * nx, 2 * nx).astype(np.float32)

    width = LANES // QG
    lane = np.zeros((QG * LANES, QG * LANES), np.float32)
    for q in range(QG):
        for i in range(planes):
            for c in range(width):
                lane[q * LANES + i * width + c, i * LANES + q * width + c] = 1.0
    comps = plane // groups
    row = np.zeros((nz * comps, nz * comps), np.float32)
    for z in range(nz):
        for r in range(comps):
            row[r * nz + z, z * comps + r] = 1.0
    return dict(
        high=high,
        low=low,
        pair=ordered(pair),
        two=ordered(two),
        lane=lane.astype(ml_dtypes.bfloat16),
        row=row.astype(ml_dtypes.bfloat16),
    )


def dot(a, b, ca=1, cb=0, precision=None):
    return lax.dot_general(
        a, b, (((ca,), (cb,)), ((), ())), precision=precision, preferred_element_type=f32
    )


def split(x):
    high = x.astype(bf16)
    return high, (x - high.astype(f32)).astype(bf16)


def dot3(a, b, ca=1, cb=0):
    (ah, al), (bh, bl) = split(a), split(b)
    return dot(ah, bh, ca, cb) + (dot(ah, bl, ca, cb) + dot(al, bh, ca, cb))


SCALE = math.sqrt(2.0 / math.pi)
CUBIC = 0.044715


def gelu(x):
    t = jnp.tanh(SCALE * (x + CUBIC * (x * x * x)))
    return 0.5 * x * (1.0 + t)


def gelu_slope(x):
    t = jnp.tanh(SCALE * (x + CUBIC * (x * x * x)))
    return 0.5 * (1.0 + t) + 0.5 * x * (1.0 - t * t) * (SCALE * (1.0 + 3.0 * CUBIC * (x * x)))


def kernel(
    nz, nc, planes,
    tokens_in, cotangent_in, up_in, down_in, filter_in, filter_out,
    plh_in, pll_in, mg_in, mt_in, lane_in, row_in,
    mixed, gtok, gup, gdn, gfi, gfo,
    a1s, a1r, a2s, a2r, a3s, a3r, a4s, a4r,
    xs, as_, fil, toks_t, cts, wts,
    mid, midg, cotg, wb, back, hid, gpre,
    gms, gmx, gmh, gmr, prs, prx, prh, prr, gw, gr1, gs, gr2,
    gfs, gfr, gfp, gfz, gfall,
    tokens, cotangent, plh, pll, mg, mt, lane, row,
    send, recv, local,
):
    ny = planes
    nh = nc // ny
    ng = nz * QG
    nb = nc // QG
    nx = nz * planes
    comps = a1s.shape[1]
    cols = comps // 2
    width, plane = wts.shape[1], mid.shape[3]
    hidden = hid.shape[0]
    z = lax.axis_index("tok")
    c = lax.axis_index("ch")
    y, h = c // nh, lax.rem(c, nh)
    b, q = c // QG, lax.rem(c, QG)
    d = z * QG + q
    core = lax.rem(c, 2)
    other = 1 - core
    sibling = c + 1 - 2 * core

    def remote(src, dst, phase, zz, cc):
        pltpu.make_async_remote_copy(
            src_ref=src, dst_ref=dst, send_sem=send.at[phase], recv_sem=recv.at[phase],
            device_id=(zz, cc), device_id_type=MESH,
        ).start()

    def here(src, dst, phase):
        pltpu.make_async_copy(src, dst, recv.at[phase]).start()

    def wait(ref, sems, phase):
        pltpu.make_async_copy(ref, ref, sems.at[phase]).wait()

    near = pl.ds(0, nc - 1)
    quarter = wb.at[0, pl.ds(0, nh)]
    small = a1s.at[pl.ds(0, ng - 1)]
    filters = gfr.at[pl.ds(0, ng - 1)]
    half = nz // 2
    brings = {
        0: a1r, 1: a2r, 2: a3r, 3: a4r, 4: quarter, 23: quarter, 5: cotg.at[:, 0], 6: quarter,
        7: midg.at[:, 0], 8: gmr, 9: prr, 10: gr1.at[0], 26: gr1.at[0], 11: gfr, 12: gr2.at[0], 27: gr2.at[0], 13: gfz,
        14: gfall.at[:, pl.ds(0, half)], 15: cotg.at[:, 0], 16: midg.at[:, 0],
        17: gmx, 18: prx, 21: quarter, 22: quarter, 24: quarter, 25: quarter, 6: quarter, 20: quarter,
    }
    brings[19] = brings[14]
    leaves = {
        0: small, 1: small, 2: small, 3: small, 5: cotg.at[near, 0], 6: quarter, 7: midg.at[near, 0],
        8: gmr.at[near], 9: prr.at[near], 10: gr1.at[0, near], 26: gr1.at[0, near], 11: filters,
        12: gr2.at[0, pl.ds(0, nz - 1)], 27: gr2.at[0, pl.ds(0, nz - 1)], 13: gfz.at[pl.ds(0, nz - 1)], 14: gfall.at[near, pl.ds(0, half)], 15: brings[15], 16: brings[16],
        17: gmx, 18: prx, 19: brings[19], 21: quarter, 22: quarter, 20: quarter, 24: quarter, 25: quarter,
    }

    def arrived(phase):
        wait(brings[phase], recv, phase)

    def left(phase):
        if phase in leaves:
            wait(leaves[phase], send, phase)
        elif phase in (4, 23):

            @pl.when(h != z)
            def _():
                wait(wb.at[0, pl.ds(0, nz)], send, phase)

            @pl.when(h == z)
            def _():
                wait(wb.at[0, pl.ds(0, nz - 1)], send, phase)

    def each(low, high, body):
        def step(k, carry):
            body(k)
            return carry
        lax.fori_loop(low, high, step, 0)

    fetches = []
    for sources in (
        ((tokens_in, tokens),), ((plh_in, plh),), ((pll_in, pll),),
        ((up_in, wts.at[0]),), ((down_in, wts.at[1]),),
        ((cotangent_in, cotangent),), ((mg_in, mg),), ((mt_in, mt),), ((lane_in, lane),),
        ((row_in, row),), ((filter_in.at[:, b], fil.at[0]),), ((filter_out.at[:, b], fil.at[1]),),
    ):
        fetches.append(
            [pltpu.make_async_copy(src, dst, local.at[len(fetches)]) for src, dst in sources]
        )
        for fetch in fetches[-1]:
            fetch.start()

    barrier = pltpu.get_barrier_semaphore()

    def greet(zz, cc):
        pl.semaphore_signal(barrier, inc=1, device_id=(zz, cc), device_id_type=MESH)

    each(1, nc, lambda k: greet(z, lax.rem(c + k, nc)))
    each(0, (nz - 1) * QG, lambda k: greet(lax.rem(z + 1 + k // QG, nz), b * QG + lax.rem(k, QG)))
    each(1, nz, lambda k: greet(lax.rem(z + k, nz), y * nh + z))

    @pl.when(h != z)
    def _():
        each(0, nh, lambda k: greet(h, y * nh + k))

    for phase in (0, 1, 2, 3, 4):
        for fetch in fetches[phase]:
            fetch.wait()
    for i in range(planes):
        toks_t[i * width:(i + 1) * width] = tokens[:, i * plane:(i + 1) * plane]

    def group_out(src, dst, phase):
        def one(k):
            dd = lax.rem(d + STRIDE * k, ng)
            remote(src.at[dd], dst.at[q, z], phase, dd // QG, b * QG + lax.rem(dd, QG))
        each(1, ng, one)
        here(src.at[d], dst.at[q, z], phase)

    def group_back(src, dst, phase):
        def one(k):
            dd = lax.rem(d + STRIDE * k, ng)
            zz, qq = dd // QG, lax.rem(dd, QG)
            remote(src.at[qq, zz], dst.at[d], phase, zz, b * QG + qq)
        each(1, ng, one)
        here(src.at[q, z], dst.at[d], phase)

    def slab_planes(src, dst, phase):
        def one(k):
            cc = lax.rem(c + STRIDE * k, nc)
            part = lax.rem(cc, 2)
            remote(src.at[cc // nh, part], dst.at[c, part], phase, z, cc)
        each(1, nc, one)
        here(src.at[y, core], dst.at[c, core], phase)

    def share(ref, phase):
        remote(ref.at[:, core], ref.at[:, core], phase, z, sibling)

    def slab_parts(src, dst, phase):
        def one(k):
            cc = lax.rem(c + STRIDE * k, nc)
            remote(src.at[cc], dst.at[c], phase, z, cc)
        each(1, nc, one)
        here(src.at[c], dst.at[c], phase)

    def plane_out(parts, dst):
        out = None
        for table, values in parts:
            term = dot(table[...], values, 1, 1)
            out = term if out is None else out + term
        dst[...] = out.astype(bf16).reshape(dst.shape)

    def plane_back(src):
        values = src[...].reshape(ng * comps, LANES)
        return dot(values, plh[...], 0, 0) + dot(values, pll[...], 0, 0)

    first_group = jnp.logical_and(z == 0, q == 0)

    def edge_table():
        return jnp.where(first_group, mt[...], mg[...])

    def evaluate(src):
        rows = nz * comps
        wide = jnp.concatenate([src[k].reshape(rows, LANES) for k in range(QG)], axis=1)
        wide = dot(wide, lane[...]).astype(bf16)
        wide = dot(row[...], wide)
        step = 2 * nz
        lines = jnp.concatenate(
            [
                jnp.concatenate(
                    [wide[k * step:(k + 1) * step, i * LANES:(i + 1) * LANES] for i in range(planes)],
                    axis=0,
                )
                for k in range(cols)
            ],
            axis=1,
        )
        edge = 2 * LANES
        first = dot(edge_table(), lines[:, :edge], precision=HIGHEST)
        rest = dot(mg[...], lines[:, edge:], precision=HIGHEST)
        spec = jnp.concatenate([first, rest], axis=1)
        mids = 2 * nx
        return jnp.concatenate(
            [
                jnp.concatenate(
                    [spec[:mids, k * LANES:(k + 1) * LANES], spec[mids:, k * LANES:(k + 1) * LANES]],
                    axis=1,
                )
                for k in range(cols)
            ],
            axis=0,
        )

    def collect(values, dst):
        mids = 2 * nx
        spec = jnp.concatenate(
            [
                jnp.concatenate(
                    [values[k * mids:(k + 1) * mids, :LANES], values[k * mids:(k + 1) * mids, LANES:]],
                    axis=0,
                )
                for k in range(cols)
            ],
            axis=1,
        )
        edge = 2 * LANES
        first = dot(edge_table(), spec[:, :edge], 0, 0, precision=HIGHEST)
        rest = dot(mg[...], spec[:, edge:], 0, 0, precision=HIGHEST)
        lines = jnp.concatenate([first, rest], axis=1)
        step = 2 * nz
        wide = jnp.concatenate(
            [
                jnp.concatenate(
                    [lines[i * step:(i + 1) * step, k * LANES:(k + 1) * LANES] for i in range(planes)],
                    axis=1,
                )
                for k in range(cols)
            ],
            axis=0,
        ).astype(bf16)
        wide = dot(row[...], wide, 0, 0).astype(bf16)
        wide = dot(wide, lane[...], 1, 1).astype(bf16)
        for k in range(QG):
            dst[k] = wide[:, k * LANES:(k + 1) * LANES].reshape(nz, comps, LANES)

    plane_out([(plh, toks_t[...]), (pll, toks_t[...])], a1s)
    pl.semaphore_wait(
        barrier, nc - 1 + (nz - 1) * QG + nz - 1 + jnp.where(h != z, nh, 0)
    )
    group_out(a1s, a1r, 0)

    wcols = y * nh + z

    def spread(part):
        def one(k):
            zz = lax.rem(z + h + k, nz)
            same = jnp.logical_and(zz == z, h == z)

            @pl.when(jnp.logical_not(same))
            def _():
                remote(wts.at[part], wb.at[part, c], (4, 23)[part], zz, wcols)

            @pl.when(same)
            def _():
                here(wts.at[part], wb.at[part, c], (4, 23)[part])
        each(0, nz, one)

    spread(0)
    spread(1)
    for fetch in fetches[5]:
        fetch.wait()
    for i in range(planes):
        cts[i] = cotangent[:, i * plane:(i + 1) * plane].reshape(2, width // 2, plane)
    slab_planes(cts, cotg, 5)

    for phase in range(6, 12):
        for fetch in fetches[phase]:
            fetch.wait()

    def complex_matrix(k):
        real, imag = fil[k, 0], fil[k, 1]
        return jnp.concatenate(
            [jnp.concatenate([real, imag], axis=1), jnp.concatenate([-imag, real], axis=1)], axis=0
        )

    arrived(0)
    x = evaluate(a1r)
    xs[...] = x
    a = dot3(x, complex_matrix(0))
    as_[...] = a
    collect(dot3(gelu(a), complex_matrix(1)), a2s)
    group_back(a2s, a2r, 1)

    after, before = lax.rem(y + 1, ny), lax.rem(y + ny - 1, ny)

    def around(part):
        arrived((4, 23)[part])
        rows = wb.at[part, pl.ds(y * nh, nh)]
        remote(rows, rows, (6, 20)[part], z, after * nh + h)
        remote(rows, rows, (21, 24)[part], z, before * nh + h)

    def onward(part):
        for k, phase, source, to in ((0, (6, 20)[part], before, after), (1, (21, 24)[part], after, before)):
            arrived(phase)
            rows = wb.at[part, pl.ds(source * nh + k * (nh // 2), nh // 2)]
            remote(rows, rows, (22, 25)[part], z, to * nh + h)

    around(0)
    arrived(5)
    share(cotg, 15)

    arrived(1)
    middle = (toks_t[...].astype(f32) + plane_back(a2r)).astype(bf16)
    mid[...] = middle.reshape(mid.shape)
    slab_planes(mid, midg, 7)
    around(1)
    onward(0)
    arrived(7)
    share(midg, 16)

    tile = min(LANES, hidden)
    chans = nc * width

    def hidden_tile(k):
        return pl.ds(pl.multiple_of(k * tile, tile), tile)

    onward(1)
    arrived(15)
    arrived(22)
    arrived(25)

    def back_step(k):
        s = hidden_tile(k)
        back[s, :] = dot(
            wb[1, :, :, s].reshape(chans, tile), cotg[...].reshape(chans, plane), 0, 0
        )
    each(0, hidden // tile, back_step)

    arrived(16)

    def pre_step(k):
        s = hidden_tile(k)
        pre = dot(wb[0, :, :, s].reshape(chans, tile), midg[...].reshape(chans, plane), 0, 0)
        hid[s, :] = gelu(pre).astype(bf16)
        gpre[s, :] = (back[s, :] * gelu_slope(pre)).astype(bf16)
    each(0, hidden // tile, pre_step)

    few = QG

    def shares(weights, values, parts, extra, phase):
        def one(k):
            s = pl.ds(k * few, few)
            part = dot(weights[s].reshape(few * width, hidden), values[...])
            parts[s] = part.astype(bf16).reshape(few, 2, width // 2, plane)
            remote(parts.at[s, other], extra.at[s], phase, z, sibling)
        each(0, nc // few, one)

    def add_pair(parts, extra, total, phase):
        arrived(phase)

        def one(k):
            s = pl.ds(k * few, few)
            total[s] = (parts[s, core].astype(f32) + extra[s].astype(f32)).astype(bf16)
        each(0, nc // few, one)

    def plane_sum(parts, i):
        halves = []
        for k in range(2):
            part = parts[i * nh + k].astype(f32)
            for j in range(k + 2, nh, 2):
                part = part + parts[i * nh + j].astype(f32)
            halves.append(part)
        return jnp.concatenate(halves, axis=0)

    shares(wb.at[0], gpre, gms, gmx, 17)

    def gw_step(k):
        s = pl.ds(k * few, few)
        part = dot(midg[s].reshape(few * width, plane), gpre[...], 1, 1)
        gw[0, s] = part.astype(bf16).reshape(few, width, hidden)
        part = dot(cotg[s].reshape(few * width, plane), hid[...], 1, 1)
        gw[1, s] = part.astype(bf16).reshape(few, width, hidden)
    each(0, nc // few, gw_step)

    add_pair(gms, gmx, gmh, 17)
    slab_parts(gmh, gmr, 8)
    slab_parts(gw.at[0], gr1.at[0], 10)
    shares(wb.at[1], hid, prs, prx, 18)

    def weight_sums(part):
        arrived((10, 26)[part])

        def one(k):
            total = gr1[part, k].astype(f32)
            for i in range(1, ny):
                total = total + gr1[part, i * nh + k].astype(f32)
            gs[part, k] = total.astype(bf16)
        each(0, nh, one)

        def out(k):
            zz = lax.rem(z + k, nz)
            remote(gs.at[part, zz], gr2.at[part, z], (12, 27)[part], zz, c)
        each(1, nz, out)
        here(gs.at[part, z], gr2.at[part, z], (12, 27)[part])

    arrived(8)
    gm = jnp.concatenate(
        [cts[i].reshape(width, plane).astype(f32) + plane_sum(gmr, i) for i in range(planes)], axis=0
    )
    high, low = split(gm)
    plane_out([(plh, high), (plh, low), (pll, high)], a3s)
    group_out(a3s, a3r, 2)

    slab_parts(gw.at[1], gr1.at[1], 26)

    arrived(2)
    dy = evaluate(a3r)
    a = as_[...]
    da = dot3(dy, complex_matrix(1), 1, 1) * gelu_slope(a)

    def fold(g):
        return g[:LANES, :LANES] + g[LANES:, LANES:], g[:LANES, LANES:] - g[LANES:, :LANES]

    in_r, in_i = fold(dot3(xs[...], da, 0, 0))
    out_r, out_i = fold(dot3(gelu(a), dy, 0, 0))
    grads = jnp.concatenate([in_r, in_i, out_r, out_i], axis=0)
    gfs[...] = grads.astype(bf16).reshape(gfs.shape)

    group_back(gfs, gfr, 11)
    collect(dot3(da, complex_matrix(0), 1, 1), a4s)
    group_back(a4s, a4r, 3)
    weight_sums(0)
    add_pair(prs, prx, prh, 18)
    slab_parts(prh, prr, 9)

    arrived(11)
    part = gfr[0].astype(f32)
    for k in range(1, ng):
        part = part + gfr[k].astype(f32)
    gfp[...] = part.astype(bf16)

    each(1, nz, lambda k: remote(gfp, gfz.at[z], 13, lax.rem(z + k, nz), c))
    here(gfp, gfz.at[z], 13)

    arrived(3)
    whole = (gm + plane_back(a4r)).astype(bf16)
    for i in range(planes):
        gtok[:, i * plane:(i + 1) * plane] = whole[i * width:(i + 1) * width]

    arrived(13)

    def gf_slab(k):
        cc = lax.rem(c + STRIDE * k, nc)
        own = pl.ds(lax.rem(cc, 2) * half, half)
        remote(gfz.at[own], gfall.at[c, own], 14, z, cc)
    each(1, nc, gf_slab)
    here(gfz.at[pl.ds(core * half, half)], gfall.at[c, pl.ds(core * half, half)], 14)
    weight_sums(1)


    arrived(14)
    own = gfall.at[:, pl.ds(core * half, half)]
    remote(own, own, 19, z, sibling)

    arrived(9)
    for i in range(planes):
        whole = mid[i].reshape(width, plane).astype(f32) + plane_sum(prr, i)
        mixed[:, i * plane:(i + 1) * plane] = whole.astype(bf16)

    for k, dst in ((0, gup), (1, gdn)):
        arrived((12, 27)[k])
        part = gr2[k, 0].astype(f32)
        for i in range(1, nz):
            part = part + gr2[k, i].astype(f32)
        dst[...] = part

    arrived(19)
    for k in range(nb):
        for j in range(QG):
            (gfi, gfo)[j // 2][j % 2, k] = gfall[k * QG + j].astype(f32).reshape(LANES, LANES)

    for phase in range(28):
        left(phase)


def solution(mesh):
    nz, nc = mesh.shape["tok"], mesh.shape["ch"]

    def local(tokens, filter_in, filter_out, up_weight, down_weight, cotangent):
        rows, width = tokens.shape
        plane = NY * NZ
        planes = rows // plane
        ng = nz * QG
        nb = nc // QG
        nh = nc // planes
        nx = nz * planes
        hidden = up_weight.shape[1]
        comps = plane // ng
        assert nh == nz and planes * width == LANES and QG * width == LANES
        tabs = tables(nz, planes)
        evals = comps // 2 * 2 * nx
        fr = 4 * LANES // ng
        halves = (nc, width // 2, plane)
        block = (nc, 2, width // 2, plane)
        out_shape = (ng, comps, LANES)
        back_shape = (QG, nz, comps, LANES)
        scratch = [
            pltpu.VMEM(shape, bf16)
            for shape in (out_shape, back_shape, back_shape, out_shape) * 2
        ] + [
            pltpu.VMEM((evals, 2 * LANES), f32),
            pltpu.VMEM((evals, 2 * LANES), f32),
            pltpu.VMEM((2, 2, LANES, LANES), f32),
            pltpu.VMEM((LANES, plane), bf16),
            pltpu.VMEM((planes, 2, width // 2, plane), bf16),
            pltpu.VMEM((2, width, hidden), bf16),
            pltpu.VMEM((planes, 2, width // 2, plane), bf16),
            pltpu.VMEM(block, bf16),
            pltpu.VMEM(block, bf16),
            pltpu.VMEM((2, nc, width, hidden), bf16),
            pltpu.VMEM((hidden, plane), f32),
            pltpu.VMEM((hidden, plane), bf16),
            pltpu.VMEM((hidden, plane), bf16),
        ] + [
            pltpu.VMEM(shape, bf16) for shape in (block, halves, halves, halves) * 2
        ] + [
            pltpu.VMEM((2, nc, width, hidden), bf16),
            pltpu.VMEM((2, nc, width, hidden), bf16),
            pltpu.VMEM((2, nh, width, hidden), bf16),
            pltpu.VMEM((2, nz, width, hidden), bf16),
            pltpu.VMEM((QG, nz, fr, LANES), bf16),
            pltpu.VMEM((ng, fr, LANES), bf16),
            pltpu.VMEM((fr, LANES), bf16),
            pltpu.VMEM((nz, fr, LANES), bf16),
            pltpu.VMEM((nc, nz, fr, LANES), bf16),
            pltpu.VMEM((width, rows), bf16),
            pltpu.VMEM((width, rows), bf16),
            pltpu.VMEM((plane, plane), bf16),
            pltpu.VMEM((plane, plane), bf16),
            pltpu.VMEM((4 * nx, 2 * nx), f32),
            pltpu.VMEM((4 * nx, 2 * nx), f32),
            pltpu.VMEM((QG * LANES, QG * LANES), bf16),
            pltpu.VMEM((nz * comps, nz * comps), bf16),
            pltpu.SemaphoreType.DMA((28,)),
            pltpu.SemaphoreType.DMA((28,)),
            pltpu.SemaphoreType.DMA((12,)),
        ]
        vmem = pl.BlockSpec(memory_space=pltpu.VMEM)
        anywhere = pl.BlockSpec(memory_space=pl.ANY)
        flops = 12 * plane * hidden * nc * width
        mixed, gtok, gup, gdn, gfi, gfo = pl.pallas_call(
            functools.partial(kernel, nz, nc, planes),
            out_shape=(
                jax.ShapeDtypeStruct((width, rows), bf16),
                jax.ShapeDtypeStruct((width, rows), bf16),
                jax.ShapeDtypeStruct((width, hidden), f32),
                jax.ShapeDtypeStruct((width, hidden), f32),
                jax.ShapeDtypeStruct(filter_in.shape, f32),
                jax.ShapeDtypeStruct(filter_out.shape, f32),
            ),
            in_specs=[anywhere] * 12,
            out_specs=[vmem] * 6,
            scratch_shapes=scratch,
            compiler_params=pltpu.CompilerParams(
                collective_id=0, has_side_effects=True, vmem_limit_bytes=60 * 2**20
            ),
            cost_estimate=pl.CostEstimate(flops=flops, bytes_accessed=2**24, transcendentals=2**20),
        )(
            tokens.T, cotangent.T, up_weight, down_weight.T, filter_in, filter_out,
            tabs["high"], tabs["low"], tabs["pair"], tabs["two"], tabs["lane"], tabs["row"],
        )

        return mixed.T, gtok.T, gup, gdn.T, gfi, gfo

    in_specs = (P("tok", "ch"), P(), P(), P("ch", "tok"), P("tok", "ch"), P("tok", "ch"))
    out_specs = (P("tok", "ch"), P("tok", "ch"), P("ch", "tok"), P("tok", "ch"), P(), P())
    return jax.shard_map(local, mesh=mesh, in_specs=in_specs, out_specs=out_specs, check_vma=False)
```

```python
import functools
import math

import jax
import jax.numpy as jnp
import ml_dtypes
import numpy as np
from jax import lax
from jax.experimental import pallas as pl
from jax.experimental.pallas import tpu as pltpu
from jax.sharding import PartitionSpec as P

NY = 64
NZ = 8
QG = 4
STRIDE = 11
LANES = 128

f32 = jnp.float32
bf16 = jnp.bfloat16
HIGHEST = lax.Precision.HIGHEST
MESH = pl.DeviceIdType.MESH


@functools.lru_cache(None)
def tables(nz, planes):
    groups = nz * QG
    nx = nz * planes
    plane = NY * NZ
    singles = [(0, 0), (0, NZ // 2), (NY // 2, 0), (NY // 2, NZ // 2)]
    pairs = []
    for v in range(NY):
        for w in range(NZ):
            other = ((-v) % NY, (-w) % NZ)
            if (v, w) < other:
                pairs.append((v, w))
    j = np.repeat(np.arange(NY), NZ)
    k = np.tile(np.arange(NZ), NY)
    rows = []
    for v, w in singles:
        rows.append(np.cos(2 * np.pi * (v * j / NY + w * k / NZ)))
    for v, w in pairs:
        angle = 2 * np.pi * (((v * j) % NY) / NY + ((w * k) % NZ) / NZ)
        rows.append(np.cos(angle))
        rows.append(-np.sin(angle))
    full = np.stack(rows) / math.sqrt(plane)
    assert full.shape == (plane, plane)
    high = full.astype(ml_dtypes.bfloat16)
    low = (full - high.astype(np.float64)).astype(ml_dtypes.bfloat16)
    u = np.arange(nx)
    turn = 2 * np.pi * ((u[:, None] * u[None, :]) % nx) / nx
    cos, sin = np.cos(turn) / math.sqrt(nx), np.sin(turn) / math.sqrt(nx)
    pair = np.zeros((2, nx, 2, 2, nx))
    pair[0, :, 0, 0], pair[0, :, 0, 1] = cos, sin
    pair[1, :, 0, 0], pair[1, :, 0, 1] = -sin, cos
    pair[0, :, 1, 0], pair[0, :, 1, 1] = cos, sin
    pair[1, :, 1, 0], pair[1, :, 1, 1] = sin, -cos
    two = np.zeros((2, nx, 2, 2, nx))
    two[0, :, 0, 0], two[1, :, 0, 0] = cos, -sin
    two[0, :, 1, 1], two[1, :, 1, 1] = cos, -sin

    def ordered(table):
        table = table.reshape(4 * nx, 2, nz, planes).transpose(0, 3, 1, 2)
        return table.reshape(4 * nx, 2 * nx).astype(np.float32)

    width = LANES // QG
    lane = np.zeros((QG * LANES, QG * LANES), np.float32)
    for q in range(QG):
        for i in range(planes):
            for c in range(width):
                lane[q * LANES + i * width + c, i * LANES + q * width + c] = 1.0
    comps = plane // groups
    row = np.zeros((nz * comps, nz * comps), np.float32)
    for z in range(nz):
        for r in range(comps):
            row[r * nz + z, z * comps + r] = 1.0
    return dict(
        high=high,
        low=low,
        pair=ordered(pair),
        two=ordered(two),
        lane=lane.astype(ml_dtypes.bfloat16),
        row=row.astype(ml_dtypes.bfloat16),
    )


def dot(a, b, ca=1, cb=0, precision=None):
    return lax.dot_general(
        a, b, (((ca,), (cb,)), ((), ())), precision=precision, preferred_element_type=f32
    )


def split(x):
    high = x.astype(bf16)
    return high, (x - high.astype(f32)).astype(bf16)


def dot3(a, b, ca=1, cb=0):
    (ah, al), (bh, bl) = split(a), split(b)
    return dot(ah, bh, ca, cb) + (dot(ah, bl, ca, cb) + dot(al, bh, ca, cb))


SCALE = math.sqrt(2.0 / math.pi)
CUBIC = 0.044715


def gelu(x):
    t = jnp.tanh(SCALE * (x + CUBIC * (x * x * x)))
    return 0.5 * x * (1.0 + t)


def gelu_slope(x):
    t = jnp.tanh(SCALE * (x + CUBIC * (x * x * x)))
    return 0.5 * (1.0 + t) + 0.5 * x * (1.0 - t * t) * (SCALE * (1.0 + 3.0 * CUBIC * (x * x)))


def kernel(
    nz, nc, planes,
    tokens_in, cotangent_in, up_in, down_in, filter_in, filter_out,
    plh_in, pll_in, mg_in, mt_in, lane_in, row_in,
    mixed, gtok, gup, gdn, gfi, gfo,
    a1s, a1r, a2s, a2r, a3s, a3r, a4s, a4r,
    xs, as_, fil, toks_t, cts, wts,
    mid, midg, cotg, wb, back, hid, gpre,
    gms, gmx, gmh, gmr, prs, prx, prh, prr, gw, gr1, gs, gr2,
    gfs, gfr, gfp, gfz, gfall,
    tokens, cotangent, plh, pll, mg, mt, lane, row,
    send, recv, local,
):
    ny = planes
    nh = nc // ny
    ng = nz * QG
    nb = nc // QG
    nx = nz * planes
    comps = a1s.shape[1]
    cols = comps // 2
    width, plane = wts.shape[1], mid.shape[3]
    hidden = hid.shape[0]
    z = lax.axis_index("tok")
    c = lax.axis_index("ch")
    y, h = c // nh, lax.rem(c, nh)
    b, q = c // QG, lax.rem(c, QG)
    d = z * QG + q
    core = lax.rem(c, 2)
    other = 1 - core
    sibling = c + 1 - 2 * core

    def remote(src, dst, phase, zz, cc):
        pltpu.make_async_remote_copy(
            src_ref=src, dst_ref=dst, send_sem=send.at[phase], recv_sem=recv.at[phase],
            device_id=(zz, cc), device_id_type=MESH,
        ).start()

    def here(src, dst, phase):
        pltpu.make_async_copy(src, dst, recv.at[phase]).start()

    def wait(ref, sems, phase):
        pltpu.make_async_copy(ref, ref, sems.at[phase]).wait()

    near = pl.ds(0, nc - 1)
    quarter = wb.at[0, pl.ds(0, nh)]
    small = a1s.at[pl.ds(0, ng - 1)]
    filters = gfr.at[pl.ds(0, ng - 1)]
    half = nz // 2
    brings = {
        0: a1r, 1: a2r, 2: a3r, 3: a4r, 4: quarter, 23: quarter, 5: cotg.at[:, 0], 6: quarter,
        7: midg.at[:, 0], 8: gmr, 9: prr, 10: gr1.at[0], 26: gr1.at[0], 11: gfr, 12: gr2.at[0], 27: gr2.at[0], 13: gfz,
        14: gfall.at[:, pl.ds(0, half)], 15: cotg.at[:, 0], 16: midg.at[:, 0],
        17: gmx, 18: prx, 21: quarter, 22: quarter, 24: quarter, 25: quarter, 6: quarter, 20: quarter,
    }
    brings[19] = brings[14]
    leaves = {
        0: small, 1: small, 2: small, 3: small, 5: cotg.at[near, 0], 6: quarter, 7: midg.at[near, 0],
        8: gmr.at[near], 9: prr.at[near], 10: gr1.at[0, near], 26: gr1.at[0, near], 11: filters,
        12: gr2.at[0, pl.ds(0, nz - 1)], 27: gr2.at[0, pl.ds(0, nz - 1)], 13: gfz.at[pl.ds(0, nz - 1)], 14: gfall.at[near, pl.ds(0, half)], 15: brings[15], 16: brings[16],
        17: gmx, 18: prx, 19: brings[19], 21: quarter, 22: quarter, 20: quarter, 24: quarter, 25: quarter,
    }

    def arrived(phase):
        wait(brings[phase], recv, phase)

    def left(phase):
        if phase in leaves:
            wait(leaves[phase], send, phase)
        elif phase in (4, 23):

            @pl.when(h != z)
            def _():
                wait(wb.at[0, pl.ds(0, nz)], send, phase)

            @pl.when(h == z)
            def _():
                wait(wb.at[0, pl.ds(0, nz - 1)], send, phase)

    def each(low, high, body):
        def step(k, carry):
            body(k)
            return carry
        lax.fori_loop(low, high, step, 0)

    fetches = []
    for sources in (
        ((tokens_in, tokens),), ((plh_in, plh),), ((pll_in, pll),),
        ((up_in, wts.at[0]),), ((down_in, wts.at[1]),),
        ((cotangent_in, cotangent),), ((mg_in, mg),), ((mt_in, mt),), ((lane_in, lane),),
        ((row_in, row),), ((filter_in.at[:, b], fil.at[0]),), ((filter_out.at[:, b], fil.at[1]),),
    ):
        fetches.append(
            [pltpu.make_async_copy(src, dst, local.at[len(fetches)]) for src, dst in sources]
        )
        for fetch in fetches[-1]:
            fetch.start()

    barrier = pltpu.get_barrier_semaphore()

    def greet(zz, cc):
        pl.semaphore_signal(barrier, inc=1, device_id=(zz, cc), device_id_type=MESH)

    each(1, nc, lambda k: greet(z, lax.rem(c + k, nc)))
    each(0, (nz - 1) * QG, lambda k: greet(lax.rem(z + 1 + k // QG, nz), b * QG + lax.rem(k, QG)))
    each(1, nz, lambda k: greet(lax.rem(z + k, nz), y * nh + z))

    @pl.when(h != z)
    def _():
        each(0, nh, lambda k: greet(h, y * nh + k))

    for phase in (0, 1, 2, 3, 4):
        for fetch in fetches[phase]:
            fetch.wait()
    for i in range(planes):
        toks_t[i * width:(i + 1) * width] = tokens[:, i * plane:(i + 1) * plane]

    def group_out(src, dst, phase):
        def one(k):
            dd = lax.rem(d + STRIDE * k, ng)
            remote(src.at[dd], dst.at[q, z], phase, dd // QG, b * QG + lax.rem(dd, QG))
        each(1, ng, one)
        here(src.at[d], dst.at[q, z], phase)

    def group_back(src, dst, phase):
        def one(k):
            dd = lax.rem(d + STRIDE * k, ng)
            zz, qq = dd // QG, lax.rem(dd, QG)
            remote(src.at[qq, zz], dst.at[d], phase, zz, b * QG + qq)
        each(1, ng, one)
        here(src.at[q, z], dst.at[d], phase)

    def slab_planes(src, dst, phase):
        def one(k):
            cc = lax.rem(c + STRIDE * k, nc)
            part = lax.rem(cc, 2)
            remote(src.at[cc // nh, part], dst.at[c, part], phase, z, cc)
        each(1, nc, one)
        here(src.at[y, core], dst.at[c, core], phase)

    def share(ref, phase):
        remote(ref.at[:, core], ref.at[:, core], phase, z, sibling)

    def slab_parts(src, dst, phase):
        def one(k):
            cc = lax.rem(c + STRIDE * k, nc)
            remote(src.at[cc], dst.at[c], phase, z, cc)
        each(1, nc, one)
        here(src.at[c], dst.at[c], phase)

    def plane_out(parts, dst):
        out = None
        for table, values in parts:
            term = dot(table[...], values, 1, 1)
            out = term if out is None else out + term
        dst[...] = out.astype(bf16).reshape(dst.shape)

    def plane_back(src):
        values = src[...].reshape(ng * comps, LANES)
        return dot(values, plh[...], 0, 0) + dot(values, pll[...], 0, 0)

    first_group = jnp.logical_and(z == 0, q == 0)

    def edge_table():
        return jnp.where(first_group, mt[...], mg[...])

    def evaluate(src):
        rows = nz * comps
        wide = jnp.concatenate([src[k].reshape(rows, LANES) for k in range(QG)], axis=1)
        wide = dot(wide, lane[...]).astype(bf16)
        wide = dot(row[...], wide)
        step = 2 * nz
        lines = jnp.concatenate(
            [
                jnp.concatenate(
                    [wide[k * step:(k + 1) * step, i * LANES:(i + 1) * LANES] for i in range(planes)],
                    axis=0,
                )
                for k in range(cols)
            ],
            axis=1,
        )
        edge = 2 * LANES
        first = dot(edge_table(), lines[:, :edge], precision=HIGHEST)
        rest = dot(mg[...], lines[:, edge:], precision=HIGHEST)
        spec = jnp.concatenate([first, rest], axis=1)
        mids = 2 * nx
        return jnp.concatenate(
            [
                jnp.concatenate(
                    [spec[:mids, k * LANES:(k + 1) * LANES], spec[mids:, k * LANES:(k + 1) * LANES]],
                    axis=1,
                )
                for k in range(cols)
            ],
            axis=0,
        )

    def collect(values, dst):
        mids = 2 * nx
        spec = jnp.concatenate(
            [
                jnp.concatenate(
                    [values[k * mids:(k + 1) * mids, :LANES], values[k * mids:(k + 1) * mids, LANES:]],
                    axis=0,
                )
                for k in range(cols)
            ],
            axis=1,
        )
        edge = 2 * LANES
        first = dot(edge_table(), spec[:, :edge], 0, 0, precision=HIGHEST)
        rest = dot(mg[...], spec[:, edge:], 0, 0, precision=HIGHEST)
        lines = jnp.concatenate([first, rest], axis=1)
        step = 2 * nz
        wide = jnp.concatenate(
            [
                jnp.concatenate(
                    [lines[i * step:(i + 1) * step, k * LANES:(k + 1) * LANES] for i in range(planes)],
                    axis=1,
                )
                for k in range(cols)
            ],
            axis=0,
        ).astype(bf16)
        wide = dot(row[...], wide, 0, 0).astype(bf16)
        wide = dot(wide, lane[...], 1, 1).astype(bf16)
        for k in range(QG):
            dst[k] = wide[:, k * LANES:(k + 1) * LANES].reshape(nz, comps, LANES)

    plane_out([(plh, toks_t[...]), (pll, toks_t[...])], a1s)
    pl.semaphore_wait(
        barrier, nc - 1 + (nz - 1) * QG + nz - 1 + jnp.where(h != z, nh, 0)
    )
    group_out(a1s, a1r, 0)

    wcols = y * nh + z

    def spread(part):
        def one(k):
            zz = lax.rem(z + h + k, nz)
            same = jnp.logical_and(zz == z, h == z)

            @pl.when(jnp.logical_not(same))
            def _():
                remote(wts.at[part], wb.at[part, c], (4, 23)[part], zz, wcols)

            @pl.when(same)
            def _():
                here(wts.at[part], wb.at[part, c], (4, 23)[part])
        each(0, nz, one)

    spread(0)
    spread(1)
    for fetch in fetches[5]:
        fetch.wait()
    for i in range(planes):
        cts[i] = cotangent[:, i * plane:(i + 1) * plane].reshape(2, width // 2, plane)
    slab_planes(cts, cotg, 5)

    for phase in range(6, 12):
        for fetch in fetches[phase]:
            fetch.wait()

    def complex_matrix(k):
        real, imag = fil[k, 0], fil[k, 1]
        return jnp.concatenate(
            [jnp.concatenate([real, imag], axis=1), jnp.concatenate([-imag, real], axis=1)], axis=0
        )

    arrived(0)
    x = evaluate(a1r)
    xs[...] = x
    a = dot3(x, complex_matrix(0))
    as_[...] = a
    collect(dot3(gelu(a), complex_matrix(1)), a2s)
    group_back(a2s, a2r, 1)

    after, before = lax.rem(y + 1, ny), lax.rem(y + ny - 1, ny)

    def around(part):
        arrived((4, 23)[part])
        rows = wb.at[part, pl.ds(y * nh, nh)]
        remote(rows, rows, (6, 20)[part], z, after * nh + h)
        remote(rows, rows, (21, 24)[part], z, before * nh + h)

    def onward(part):
        for k, phase, source, to in ((0, (6, 20)[part], before, after), (1, (21, 24)[part], after, before)):
            arrived(phase)
            rows = wb.at[part, pl.ds(source * nh + k * (nh // 2), nh // 2)]
            remote(rows, rows, (22, 25)[part], z, to * nh + h)

    around(0)
    arrived(5)
    share(cotg, 15)

    arrived(1)
    middle = (toks_t[...].astype(f32) + plane_back(a2r)).astype(bf16)
    mid[...] = middle.reshape(mid.shape)
    slab_planes(mid, midg, 7)
    around(1)
    onward(0)
    arrived(7)
    share(midg, 16)

    tile = min(LANES, hidden)
    chans = nc * width

    def hidden_tile(k):
        return pl.ds(pl.multiple_of(k * tile, tile), tile)

    onward(1)
    arrived(15)
    arrived(22)
    arrived(25)

    def back_step(k):
        s = hidden_tile(k)
        back[s, :] = dot(
            wb[1, :, :, s].reshape(chans, tile), cotg[...].reshape(chans, plane), 0, 0
        )
    each(0, hidden // tile, back_step)

    arrived(16)

    def pre_step(k):
        s = hidden_tile(k)
        pre = dot(wb[0, :, :, s].reshape(chans, tile), midg[...].reshape(chans, plane), 0, 0)
        hid[s, :] = gelu(pre).astype(bf16)
        gpre[s, :] = (back[s, :] * gelu_slope(pre)).astype(bf16)
    each(0, hidden // tile, pre_step)

    few = QG

    def shares(weights, values, parts, extra, phase):
        def one(k):
            s = pl.ds(k * few, few)
            part = dot(weights[s].reshape(few * width, hidden), values[...])
            parts[s] = part.astype(bf16).reshape(few, 2, width // 2, plane)
            remote(parts.at[s, other], extra.at[s], phase, z, sibling)
        each(0, nc // few, one)

    def add_pair(parts, extra, total, phase):
        arrived(phase)

        def one(k):
            s = pl.ds(k * few, few)
            total[s] = (parts[s, core].astype(f32) + extra[s].astype(f32)).astype(bf16)
        each(0, nc // few, one)

    def plane_sum(parts, i):
        halves = []
        for k in range(2):
            part = parts[i * nh + k].astype(f32)
            for j in range(k + 2, nh, 2):
                part = part + parts[i * nh + j].astype(f32)
            halves.append(part)
        return jnp.concatenate(halves, axis=0)

    shares(wb.at[0], gpre, gms, gmx, 17)

    def weight_terms(part, left_side, right_side):
        def one(k):
            s = pl.ds(k * few, few)
            term = dot(left_side[s].reshape(few * width, plane), right_side[...], 1, 1)
            gw[part, s] = term.astype(bf16).reshape(few, width, hidden)
        each(0, nc // few, one)
        slab_parts(gw.at[part], gr1.at[part], (10, 26)[part])

    add_pair(gms, gmx, gmh, 17)
    slab_parts(gmh, gmr, 8)
    weight_terms(0, midg, gpre)
    shares(wb.at[1], hid, prs, prx, 18)

    def weight_sums(part):
        arrived((10, 26)[part])

        def one(k):
            total = gr1[part, k].astype(f32)
            for i in range(1, ny):
                total = total + gr1[part, i * nh + k].astype(f32)
            gs[part, k] = total.astype(bf16)
        each(0, nh, one)

        def out(k):
            zz = lax.rem(z + k, nz)
            remote(gs.at[part, zz], gr2.at[part, z], (12, 27)[part], zz, c)
        each(1, nz, out)
        here(gs.at[part, z], gr2.at[part, z], (12, 27)[part])

    arrived(8)
    gm = jnp.concatenate(
        [cts[i].reshape(width, plane).astype(f32) + plane_sum(gmr, i) for i in range(planes)], axis=0
    )
    high, low = split(gm)
    plane_out([(plh, high), (plh, low), (pll, high)], a3s)
    group_out(a3s, a3r, 2)

    weight_terms(1, cotg, hid)

    arrived(2)
    dy = evaluate(a3r)
    a = as_[...]
    da = dot3(dy, complex_matrix(1), 1, 1) * gelu_slope(a)

    def fold(g):
        return g[:LANES, :LANES] + g[LANES:, LANES:], g[:LANES, LANES:] - g[LANES:, :LANES]

    in_r, in_i = fold(dot3(xs[...], da, 0, 0))
    out_r, out_i = fold(dot3(gelu(a), dy, 0, 0))
    grads = jnp.concatenate([in_r, in_i, out_r, out_i], axis=0)
    gfs[...] = grads.astype(bf16).reshape(gfs.shape)

    group_back(gfs, gfr, 11)
    collect(dot3(da, complex_matrix(0), 1, 1), a4s)
    group_back(a4s, a4r, 3)
    weight_sums(0)
    add_pair(prs, prx, prh, 18)
    slab_parts(prh, prr, 9)

    arrived(11)
    part = gfr[0].astype(f32)
    for k in range(1, ng):
        part = part + gfr[k].astype(f32)
    gfp[...] = part.astype(bf16)

    each(1, nz, lambda k: remote(gfp, gfz.at[z], 13, lax.rem(z + k, nz), c))
    here(gfp, gfz.at[z], 13)

    arrived(3)
    whole = (gm + plane_back(a4r)).astype(bf16)
    for i in range(planes):
        gtok[:, i * plane:(i + 1) * plane] = whole[i * width:(i + 1) * width]

    arrived(13)

    def gf_slab(k):
        cc = lax.rem(c + STRIDE * k, nc)
        own = pl.ds(lax.rem(cc, 2) * half, half)
        remote(gfz.at[own], gfall.at[c, own], 14, z, cc)
    each(1, nc, gf_slab)
    here(gfz.at[pl.ds(core * half, half)], gfall.at[c, pl.ds(core * half, half)], 14)
    weight_sums(1)


    arrived(14)
    own = gfall.at[:, pl.ds(core * half, half)]
    remote(own, own, 19, z, sibling)

    arrived(9)
    for i in range(planes):
        whole = mid[i].reshape(width, plane).astype(f32) + plane_sum(prr, i)
        mixed[:, i * plane:(i + 1) * plane] = whole.astype(bf16)

    for k, dst in ((0, gup), (1, gdn)):
        arrived((12, 27)[k])
        part = gr2[k, 0].astype(f32)
        for i in range(1, nz):
            part = part + gr2[k, i].astype(f32)
        dst[...] = part

    arrived(19)
    for k in range(nb):
        for j in range(QG):
            (gfi, gfo)[j // 2][j % 2, k] = gfall[k * QG + j].astype(f32).reshape(LANES, LANES)

    for phase in range(28):
        left(phase)


def solution(mesh):
    nz, nc = mesh.shape["tok"], mesh.shape["ch"]

    def local(tokens, filter_in, filter_out, up_weight, down_weight, cotangent):
        rows, width = tokens.shape
        plane = NY * NZ
        planes = rows // plane
        ng = nz * QG
        nb = nc // QG
        nh = nc // planes
        nx = nz * planes
        hidden = up_weight.shape[1]
        comps = plane // ng
        assert nh == nz and planes * width == LANES and QG * width == LANES
        tabs = tables(nz, planes)
        evals = comps // 2 * 2 * nx
        fr = 4 * LANES // ng
        halves = (nc, width // 2, plane)
        block = (nc, 2, width // 2, plane)
        out_shape = (ng, comps, LANES)
        back_shape = (QG, nz, comps, LANES)
        scratch = [
            pltpu.VMEM(shape, bf16)
            for shape in (out_shape, back_shape, back_shape, out_shape) * 2
        ] + [
            pltpu.VMEM((evals, 2 * LANES), f32),
            pltpu.VMEM((evals, 2 * LANES), f32),
            pltpu.VMEM((2, 2, LANES, LANES), f32),
            pltpu.VMEM((LANES, plane), bf16),
            pltpu.VMEM((planes, 2, width // 2, plane), bf16),
            pltpu.VMEM((2, width, hidden), bf16),
            pltpu.VMEM((planes, 2, width // 2, plane), bf16),
            pltpu.VMEM(block, bf16),
            pltpu.VMEM(block, bf16),
            pltpu.VMEM((2, nc, width, hidden), bf16),
            pltpu.VMEM((hidden, plane), f32),
            pltpu.VMEM((hidden, plane), bf16),
            pltpu.VMEM((hidden, plane), bf16),
        ] + [
            pltpu.VMEM(shape, bf16) for shape in (block, halves, halves, halves) * 2
        ] + [
            pltpu.VMEM((2, nc, width, hidden), bf16),
            pltpu.VMEM((2, nc, width, hidden), bf16),
            pltpu.VMEM((2, nh, width, hidden), bf16),
            pltpu.VMEM((2, nz, width, hidden), bf16),
            pltpu.VMEM((QG, nz, fr, LANES), bf16),
            pltpu.VMEM((ng, fr, LANES), bf16),
            pltpu.VMEM((fr, LANES), bf16),
            pltpu.VMEM((nz, fr, LANES), bf16),
            pltpu.VMEM((nc, nz, fr, LANES), bf16),
            pltpu.VMEM((width, rows), bf16),
            pltpu.VMEM((width, rows), bf16),
            pltpu.VMEM((plane, plane), bf16),
            pltpu.VMEM((plane, plane), bf16),
            pltpu.VMEM((4 * nx, 2 * nx), f32),
            pltpu.VMEM((4 * nx, 2 * nx), f32),
            pltpu.VMEM((QG * LANES, QG * LANES), bf16),
            pltpu.VMEM((nz * comps, nz * comps), bf16),
            pltpu.SemaphoreType.DMA((28,)),
            pltpu.SemaphoreType.DMA((28,)),
            pltpu.SemaphoreType.DMA((12,)),
        ]
        vmem = pl.BlockSpec(memory_space=pltpu.VMEM)
        anywhere = pl.BlockSpec(memory_space=pl.ANY)
        flops = 12 * plane * hidden * nc * width
        mixed, gtok, gup, gdn, gfi, gfo = pl.pallas_call(
            functools.partial(kernel, nz, nc, planes),
            out_shape=(
                jax.ShapeDtypeStruct((width, rows), bf16),
                jax.ShapeDtypeStruct((width, rows), bf16),
                jax.ShapeDtypeStruct((width, hidden), f32),
                jax.ShapeDtypeStruct((width, hidden), f32),
                jax.ShapeDtypeStruct(filter_in.shape, f32),
                jax.ShapeDtypeStruct(filter_out.shape, f32),
            ),
            in_specs=[anywhere] * 12,
            out_specs=[vmem] * 6,
            scratch_shapes=scratch,
            compiler_params=pltpu.CompilerParams(
                collective_id=0, has_side_effects=True, vmem_limit_bytes=60 * 2**20
            ),
            cost_estimate=pl.CostEstimate(flops=flops, bytes_accessed=2**24, transcendentals=2**20),
        )(
            tokens.T, cotangent.T, up_weight, down_weight.T, filter_in, filter_out,
            tabs["high"], tabs["low"], tabs["pair"], tabs["two"], tabs["lane"], tabs["row"],
        )

        return mixed.T, gtok.T, gup, gdn.T, gfi, gfo

    in_specs = (P("tok", "ch"), P(), P(), P("ch", "tok"), P("tok", "ch"), P("tok", "ch"))
    out_specs = (P("tok", "ch"), P("tok", "ch"), P("ch", "tok"), P("tok", "ch"), P(), P())
    return jax.shard_map(local, mesh=mesh, in_specs=in_specs, out_specs=out_specs, check_vma=False)
```
